32 devices in a mesh: dp: 4 (over z), row: 4 (over y, core), col: 2 (over x).
Axes of the slice: x: 2, y: 2, z: 4, core: 2. Of those that a mesh axis runs over, the one named last changes fastest.
Arguments:
- grad_wi: bfloat16 [4, 4096, 16384], P('dp', 'row', 'col'), may hold values from -100 to 100
- grad_wo: bfloat16 [4, 16384, 4096], P('dp', 'row', 'col'), may hold values from -100 to 100
- row_wi: float32 [4096], P('row'), may hold values from 0.01 to 1
- col_wi: float32 [16384], P('col'), may hold values from 0.01 to 1
- row_wo: float32 [16384], P('row'), may hold values from 0.01 to 1
- col_wo: float32 [4096], P('col'), may hold values from 0.01 to 1
Outputs:
- update_wi: bfloat16 [4096, 16384], P('row', 'col')
- row_wi_new: float32 [4096], P('row')
- col_wi_new: float32 [16384], P('col')
- update_wo: bfloat16 [16384, 4096], P('row', 'col')
- row_wo_new: float32 [16384], P('row')
- col_wo_new: float32 [4096], P('col')
The draws below stay inside these ranges and needn't reach their ends.
All inputs are finite; a program needn't handle non-finite values.
Results may differ from the reference program's by a relative error of at most 0.015.
Values may be sent and summed in bfloat16 or wider, within the bound.
No kernel may reach another device: no remote copies, remote signals or barrier semaphores. Data moves between devices by JAX's collectives and lax.ppermute only.
A program may use at most 192 MiB of HBM per device.

```python
import math
import jax
import jax.numpy as jnp
from jax import lax

D = 4096
FF = 16384
N_DP = 4


LOG_HOT = 2.77


def tile_levels(key, count):
    tile_draws = jax.random.uniform(key, (count // 64,), jnp.float32, 0.0, 1.0)
    hot_level = jnp.clip(3.0 * tile_draws - 1.0, 0.0, 1.0)
    return jnp.repeat(hot_level, 64)


def make_gradient(key, groups, rows, cols):
    keys = jax.random.split(key, 7)
    ramp_rows = jnp.sqrt(1.0 + 2.0 * jnp.arange(rows, dtype=jnp.float32) / rows)
    ramp_cols = jnp.sqrt(1.0 + 2.0 * jnp.arange(cols, dtype=jnp.float32) / cols)
    row_scale = jnp.exp(jax.random.uniform(keys[0], (rows,), jnp.float32, -0.9, 0.9)) * ramp_rows
    col_scale = jnp.exp(jax.random.uniform(keys[1], (cols,), jnp.float32, -0.9, 0.9)) * ramp_cols
    row_level = tile_levels(keys[5], rows)
    col_level = tile_levels(keys[6], cols)
    joint_factor = jnp.exp(0.5 * LOG_HOT * row_level[:, None] * col_level[None, :])
    noise = jnp.clip(jax.random.normal(keys[2], (groups, rows, cols), jnp.float32), -5.0, 5.0)
    values = 0.2 * noise * row_scale[None, :, None] * col_scale[None, None, :] * joint_factor[None, :, :]
    values = jnp.clip(values, -100.0, 100.0)
    return values.astype(jnp.bfloat16)


def draw_grad_wi(key, part):
    return make_gradient(jax.random.fold_in(key, 11), N_DP, D, FF)


def draw_grad_wo(key, part):
    return make_gradient(jax.random.fold_in(key, 23), N_DP, FF, D)


def steps_of(own_key, dims, pieces, least, largest):
    gain = 1.0
    for axis_at, shards_of in pieces:
        draws = jax.random.uniform(jax.random.fold_in(jax.random.fold_in(own_key, 6), axis_at), (shards_of,), jnp.float32, least / len(pieces), largest / len(pieces))
        gain = gain * jnp.repeat(jnp.exp(draws), dims[axis_at] // shards_of).reshape((-1,) + (1,) * (len(dims) - 1 - axis_at))
    return gain


def setup_inputs(seed: int = 0) -> dict:
    seeds = jax.random.split(jax.random.key(seed), 7)
    return {
        "grad_wi": draw_grad_wi(jax.random.fold_in(seeds[6], 71), 0),
        "grad_wo": draw_grad_wo(jax.random.fold_in(seeds[6], 71), 0),
        "row_wi": jnp.clip(jnp.exp(math.log(1.0) - 4.6051702 * jax.random.uniform(seeds[2], (D,), jnp.float32) ** steps_of(seeds[2], (D,), ((0, 4),), -0.2, 0.2)), 0.01, 1.0),
        "col_wi": jnp.clip(jnp.exp(math.log(1.0) - 4.6051702 * jax.random.uniform(seeds[3], (FF,), jnp.float32) ** steps_of(seeds[3], (FF,), ((0, 2),), -0.2, 0.2)), 0.01, 1.0),
        "row_wo": jnp.clip(jnp.exp(math.log(1.0) - 4.6051702 * jax.random.uniform(seeds[4], (FF,), jnp.float32) ** steps_of(seeds[4], (FF,), ((0, 4),), -0.2, 0.2)), 0.01, 1.0),
        "col_wo": jnp.clip(jnp.exp(math.log(1.0) - 4.6051702 * jax.random.uniform(seeds[5], (D,), jnp.float32) ** steps_of(seeds[5], (D,), ((0, 2),), -0.2, 0.2)), 0.01, 1.0),
    }


BETA = 0.8
EPS_SQUARE = 1e-30

def factored(grad, row_prev, col_prev):
    total = lax.optimization_barrier(jnp.sum(grad.astype(jnp.float32), axis=0))
    squares = total * total + EPS_SQUARE
    row_new = BETA * row_prev + (1.0 - BETA) * lax.optimization_barrier(jnp.mean(squares, axis=1))
    col_new = BETA * col_prev + (1.0 - BETA) * lax.optimization_barrier(jnp.mean(squares, axis=0))
    second = row_new[:, None] * col_new[None, :]
    raw = total / jnp.sqrt(second)
    rms_value = jnp.sqrt(jnp.mean(raw * raw))
    update = (raw / jnp.maximum(1.0, rms_value)).astype(jnp.bfloat16)
    return (update, row_new, col_new)

def reference(grad_wi, grad_wo, row_wi, col_wi, row_wo, col_wo):
    update_wi, row_wi_new, col_wi_new = factored(grad_wi, row_wi, col_wi)
    update_wo, row_wo_new, col_wo_new = factored(grad_wo, row_wo, col_wo)
    return (update_wi, row_wi_new, col_wi_new, update_wo, row_wo_new, col_wo_new)
```

```python
import jax
import jax.numpy as jnp
from jax import lax
from jax.sharding import PartitionSpec as P

BETA = 0.8
EPS_SQUARE = 1e-30
CHUNKS = 16
LAG = 2


def chunk_count(rows):
    half = rows // 2
    count = CHUNKS
    while half % count or (half // count) % 8:
        count //= 2
    return count


def make_local(n_dp, n_row, n_col):
    last = n_dp - 1

    def local(grad_wi, grad_wo, row_wi, col_wi, row_wo, col_wo):
        f32, bf16 = jnp.float32, jnp.bfloat16
        place = lax.axis_index("dp")
        grads = (grad_wi[0], grad_wo[0])
        prevs = ((row_wi, col_wi), (row_wo, col_wo))
        shapes = [g.shape for g in grads]
        counts = [chunk_count(rows) for rows, _ in shapes]
        sizes = [rows // 2 // count for (rows, _), count in zip(shapes, counts)]

        position = (place, last - place)
        at_end = (place == last) | (place == 0)

        segments = []
        start = 0
        for kind in ("sum", "spread"):
            for m in range(2):
                segments.append((kind, m, start))
                start += counts[m]
        steps = start + LAG * last

        def hop(value, direction, senders):
            pairs = []
            for p in senders:
                if p < last:
                    pairs.append((p, p + 1) if direction == 0 else (last - p, last - p - 1))
            return lax.ppermute(value, "dp", pairs) if pairs else None

        inflight = {}
        finals = {(m, d): [] for m in range(2) for d in range(2)}
        latest = {}
        updates = {}
        outs = [jnp.zeros(shape, bf16) for shape in shapes]
        results = {}

        def statistics(m):
            rows, cols = shapes[m]
            half = rows // 2
            total = jnp.concatenate(
                [jnp.where(place == 0, low, high) for high, low in zip(finals[m, 0], finals[m, 1])]
            )
            if updates:
                total, _ = lax.optimization_barrier((total, updates[m - 1][3]))
            wide = total.astype(f32)
            square = wide * wide + EPS_SQUARE
            row_part = jnp.sum(square, axis=1)
            col_part = jnp.sum(square, axis=0)
            row_all = jnp.concatenate(
                [jnp.where(place == last, row_part, 0.0), jnp.where(place == 0, row_part, 0.0)]
            )
            row_sum = lax.psum(row_all, ("dp", "col"))
            col_sum = lax.psum(jnp.where(at_end, col_part, 0.0), ("dp", "row"))
            row_new = BETA * prevs[m][0] + (1.0 - BETA) * (row_sum / (cols * n_col))
            col_new = BETA * prevs[m][1] + (1.0 - BETA) * (col_sum / (rows * n_row))
            row_half = jnp.where(place == 0, row_new[half:], row_new[:half])
            row_scale = lax.rsqrt(row_half)
            col_scale = lax.rsqrt(col_new)
            raw = wide * row_scale[:, None] * col_scale[None, :]
            energy = lax.psum(jnp.where(at_end, jnp.sum(raw * raw), 0.0), ("dp", "row", "col"))
            rms = jnp.sqrt(energy / (rows * n_row * cols * n_col))
            row_final = row_scale / jnp.maximum(1.0, rms)
            updates[m] = (raw_update(total, row_final, col_scale), row_new, col_new, energy)

        def raw_update(total, row_final, col_scale):
            wide = total.astype(f32)
            return (wide * row_final[:, None] * col_scale[None, :]).astype(bf16)

        arrived = {}
        tied = {}
        for s in range(steps):
            batch = []
            for index, (kind, m, begin) in enumerate(segments):
                members = [p for p in range(n_dp) if 0 <= s - LAG * p - begin < counts[m]]
                if not members:
                    continue
                size = sizes[m]
                half = shapes[m][0] // 2
                cols = shapes[m][1]
                if kind == "spread" and m not in updates:
                    statistics(m)
                for d in range(2):
                    got = inflight.pop((index, d, s - LAG), None)
                    at = jnp.clip(s - begin - LAG * position[d], 0, counts[m] - 1) * size
                    if kind == "sum":
                        own = lax.dynamic_slice(grads[m], (d * half + at, 0), (size, cols))
                        value = own
                        if got is not None:
                            value = (got.astype(f32) + own.astype(f32)).astype(bf16)
                        if last in members:
                            finals[m, d].append(value)
                    else:
                        value = got
                        if 0 in members:
                            k = s - begin
                            mine = updates[m][0][k * size : (k + 1) * size]
                            value = mine if got is None else jnp.where(position[d] == 0, mine, got)
                        elif got is not None:
                            done = s - LAG * position[d] - begin >= counts[m]
                            value = jnp.where(done, latest[m, d], got)
                        latest[m, d] = value
                        outs[m] = lax.dynamic_update_slice(
                            outs[m], value, ((1 - d) * half + at, 0)
                        )
                    if min(members) < last:
                        batch.append((index, d, members, value))
            values = [value for _, _, _, value in batch]
            after = arrived.get(s - LAG, []) + tied.get(s - 1, [])
            if values:
                values, _ = lax.optimization_barrier((values, after))
            tied[s] = values
            arrived[s] = []
            for (index, d, members, _), value in zip(batch, values):
                inflight[index, d, s] = hop(value, d, members)
                arrived[s].append(inflight[index, d, s])
        return (outs[0], updates[0][1], updates[0][2], outs[1], updates[1][1], updates[1][2])

    return local


def solution(mesh):
    sizes = mesh.shape
    return jax.shard_map(
        make_local(sizes["dp"], sizes["row"], sizes["col"]),
        mesh=mesh,
        in_specs=(
            P("dp", "row", "col"),
            P("dp", "row", "col"),
            P("row"),
            P("col"),
            P("row"),
            P("col"),
        ),
        out_specs=(P("row", "col"), P("row"), P("col"), P("row", "col"), P("row"), P("col")),
        check_vma=False,
    )
```

```python
import jax
import jax.numpy as jnp
from jax import lax
from jax.sharding import PartitionSpec as P

BETA = 0.8
EPS_SQUARE = 1e-30
CHUNKS = 32
LAG = 2
GROUPS = 4
FAR = 3


def chunk_count(rows):
    half = rows // 2
    count = CHUNKS
    while half % count or (half // count) % 8:
        count //= 2
    return count


def make_local(axis_sizes):
    n_dp, n_row, n_col = axis_sizes["dp"], axis_sizes["row"], axis_sizes["col"]
    last = n_dp - 1

    def spread_ends(value):
        total = value
        for j in range(1, n_dp):
            pairs = [[(0, j)], [(last, last - j)]]
            if j != last - j:
                pairs = [pairs[0] + pairs[1]]
            for some in pairs:
                total = total + lax.ppermute(value, "dp", some)
        return total

    def butterfly(value, axis, distance):
        n = axis_sizes[axis]
        return value + lax.ppermute(value, axis, [(i, i ^ distance) for i in range(n)])

    def distances(axis):
        out, d = [], 1
        while d < axis_sizes[axis]:
            out.append(d)
            d *= 2
        return out

    def local(grad_wi, grad_wo, row_wi, col_wi, row_wo, col_wo):
        f32, bf16 = jnp.float32, jnp.bfloat16
        place = lax.axis_index("dp")
        grads = (grad_wi[0], grad_wo[0])
        prevs = ((row_wi, col_wi), (row_wo, col_wo))
        shapes = [g.shape for g in grads]
        counts = [chunk_count(rows) for rows, _ in shapes]
        sizes = [rows // 2 // count for (rows, _), count in zip(shapes, counts)]

        at_end = (place == last) | (place == 0)

        segments = []
        start = 0
        for kind in ("sum", "spread"):
            for m in range(2):
                segments.append((kind, m, start))
                start += counts[m]
        steps = start + LAG * last

        def hop(value, direction, senders):
            pairs = []
            for p in senders:
                if p < last:
                    pairs.append((p, p + 1) if direction == 0 else (last - p, last - p - 1))
            return lax.ppermute(value, "dp", pairs)

        held = {0: [], 1: []}
        scales = {}
        results = {}
        cell = [None]

        def settle(value):
            value, _ = lax.optimization_barrier((value, cell[0]))
            return value

        def group_of(m, g):
            per = counts[m] // GROUPS
            return jnp.concatenate(held[m][g * per : (g + 1) * per])

        def statistics(m):
            rows, cols = shapes[m]
            half = rows // 2
            per = counts[m] // GROUPS
            row_parts, col_part = [], None
            for g in range(GROUPS):
                while len(held[m]) < (g + 1) * per:
                    yield [], 1
                wide = settle(group_of(m, g)).astype(f32)
                square = wide * wide + EPS_SQUARE
                row_parts.append(jnp.sum(square, axis=1))
                part = jnp.sum(square, axis=0)
                col_part = part if col_part is None else col_part + part
                yield [row_parts[-1], col_part], 1
            row_part = jnp.concatenate(row_parts)
            levels = max(len(distances("row")), len(distances("col")))
            for level in range(levels):
                row_part, col_part = settle((row_part, col_part))
                if level < len(distances("col")):
                    row_part = butterfly(row_part, "col", distances("col")[level])
                if level < len(distances("row")):
                    col_part = butterfly(col_part, "row", distances("row")[level])
                yield [], 1
            row_part, col_part = settle((row_part, col_part))
            packed = jnp.concatenate(
                [
                    jnp.where(place == last, row_part, 0.0),
                    jnp.where(place == 0, row_part, 0.0),
                    jnp.where(at_end, col_part, 0.0),
                ]
            )
            packed = spread_ends(packed)
            yield [], FAR
            packed = settle(packed)
            row_new = BETA * prevs[m][0] + (1.0 - BETA) * (packed[:rows] / (cols * n_col))
            col_new = BETA * prevs[m][1] + (1.0 - BETA) * (packed[rows:] / (rows * n_row))
            row_scale = lax.rsqrt(jnp.where(place == 0, row_new[half:], row_new[:half]))
            col_scale = lax.rsqrt(col_new)
            yield [row_scale, col_scale], 1
            energy = None
            for g in range(GROUPS):
                own_rows = row_scale[g * half // GROUPS : (g + 1) * half // GROUPS]
                wide = settle(group_of(m, g)).astype(f32)
                raw = wide * own_rows[:, None] * col_scale[None, :]
                part = jnp.sum(raw * raw)
                energy = part if energy is None else energy + part
                yield [energy], 1
            energy = jnp.broadcast_to(energy, (8, 128))
            for axis in ("col", "row"):
                for distance in distances(axis):
                    energy = butterfly(settle(energy), axis, distance)
                    yield [], 1
            energy = settle(energy)
            energy = energy + lax.ppermute(energy, "dp", [(0, last), (last, 0)])
            yield [], FAR
            energy = settle(energy)[0, 0]
            rms = jnp.sqrt(energy / (rows * n_row * cols * n_col))
            row_final = row_scale / jnp.maximum(1.0, rms)
            scales[m] = (row_final, col_scale)
            results[m] = (row_new, col_new)
            yield [row_final], 1

        workers = [statistics(0), statistics(1)]
        wakes = [0, 0]

        def advance(m):
            try:
                ties, wait = next(workers[m])
            except StopIteration:
                return [], steps
            return ties, wait

        outs = [jnp.zeros(shape, bf16) for shape in shapes]
        inflight = {}
        latest = {}
        arrived = {}
        tied = []
        for s in range(steps):
            active = []
            for index, (kind, m, begin) in enumerate(segments):
                members = [p for p in range(n_dp) if 0 <= s - LAG * p - begin < counts[m]]
                if members:
                    active.append((index, kind, m, begin, members))
                if members and kind == "spread" and m not in scales:
                    while m not in scales:
                        advance(m)
                    wakes[m] = steps
            gots = [
                inflight.pop((index, d, s - LAG), None)
                for index, _, _, _, _ in active
                for d in range(2)
            ]
            here = place
            position = (here, last - here)
            before, tied = tied, []
            batch = []
            turn = 0
            for index, kind, m, begin, members in active:
                size = sizes[m]
                half = shapes[m][0] // 2
                cols = shapes[m][1]
                ending = {}
                for d in range(2):
                    got = gots[turn]
                    turn += 1
                    at = jnp.clip(s - begin - LAG * position[d], 0, counts[m] - 1) * size
                    if kind == "sum":
                        own = lax.dynamic_slice(grads[m], (d * half + at, 0), (size, cols))
                        value = own
                        if got is not None:
                            value = (got.astype(f32) + own.astype(f32)).astype(bf16)
                        ending[d] = value
                    else:
                        value = got
                        if 0 in members:
                            k = s - begin
                            per = counts[m] // GROUPS
                            low = (k % per) * size
                            row_final, col_scale = scales[m]
                            wide = group_of(m, k // per)[low : low + size].astype(f32)
                            rows_here = row_final[k * size : (k + 1) * size]
                            mine = (wide * rows_here[:, None] * col_scale[None, :]).astype(bf16)
                            value = mine if got is None else jnp.where(position[d] == 0, mine, got)
                        elif got is not None:
                            done = s - LAG * position[d] - begin >= counts[m]
                            value = jnp.where(done, latest[m, d], got)
                        latest[m, d] = value
                        outs[m] = lax.dynamic_update_slice(
                            outs[m], value, ((1 - d) * half + at, 0)
                        )
                    if min(members) < last:
                        batch.append((index, d, members, value))
                        tied.append(value)
                if kind == "sum" and last in members:
                    held[m].append(jnp.where(here == 0, ending[1], ending[0]))
            if batch:
                values, _ = lax.optimization_barrier(([b[3] for b in batch], (before, arrived.get(s - LAG, []))))
                tied = list(values)
            arrived[s] = []
            for (index, d, members, _), value in zip(batch, tied):
                inflight[index, d, s] = hop(value, d, members)
                arrived[s].append(inflight[index, d, s])
            cell[0] = list(tied)
            for m in range(2):
                if s >= wakes[m]:
                    ties, wait = advance(m)
                    tied = tied + ties
                    wakes[m] = s + wait
        return (outs[0], *results[0], outs[1], *results[1])

    return local


def solution(mesh):
    return jax.shard_map(
        make_local(dict(mesh.shape)),
        mesh=mesh,
        in_specs=(
            P("dp", "row", "col"),
            P("dp", "row", "col"),
            P("row"),
            P("col"),
            P("row"),
            P("col"),
        ),
        out_specs=(P("row", "col"), P("row"), P("col"), P("row", "col"), P("row"), P("col")),
        check_vma=False,
    )
```

```python
import functools

import jax
import jax.numpy as jnp
from jax import lax
from jax.experimental import pallas as pl
from jax.experimental.pallas import tpu as pltpu
from jax.sharding import PartitionSpec as P

BETA = 0.8
EPS_SQUARE = 1e-30
CHUNKS = 16
LAG = 2
GROUPS = 4
FAR = 2
LANES = 128

F32 = jnp.float32
BF16 = jnp.bfloat16
ANY = pl.BlockSpec(memory_space=pl.ANY)


def chunk_count(rows):
    half = rows // 2
    count = CHUNKS
    while half % count or (half // count) % 16:
        count //= 2
    return count


def block_rows(size, cols):
    rows = size
    while rows % 32 == 0 and rows * cols > 16 * 8192:
        rows //= 2
    return rows


def sum_kernel(with_got, with_total, first_total, at_ref, *refs):
    refs = list(refs)
    gots = [refs.pop(0), refs.pop(0)] if with_got else [None, None]
    owns = [refs.pop(0), refs.pop(0)]
    if with_total and not first_total:
        refs.pop(0)
        refs.pop(0)
        col_in = refs.pop(0)
    sends = [refs.pop(0), refs.pop(0)]
    rows, cols = sends[0].shape
    low_end = at_ref[2] == 0
    if with_total:
        total_ref, row_ref, col_ref = refs

        @pl.when(pl.program_id(0) == 0)
        def _():
            col_ref[...] = jnp.zeros(col_ref.shape, F32) if first_total else col_in[...]

    row_part = jnp.zeros((rows, LANES), F32)
    for j in range(cols // LANES):
        lanes = pl.ds(j * LANES, LANES)
        values = []
        for got, own, send in zip(gots, owns, sends):
            value = own[:, lanes]
            if got is not None:
                value = (got[:, lanes].astype(F32) + value.astype(F32)).astype(BF16)
            send[:, lanes] = value
            values.append(value)
        if with_total:
            total = jnp.where(low_end, values[1], values[0])
            total_ref[:, lanes] = total
            wide = total.astype(F32)
            square = wide * wide + EPS_SQUARE
            row_part = row_part + square
            col_part = square[0:8]
            for r in range(8, rows, 8):
                col_part = col_part + square[r : r + 8]
            col_ref[:, lanes] += col_part
    if with_total:
        row_ref[...] = row_part


def sum_step(at, gots, grad, size, chunk, count, state):
    rows, cols = grad.shape
    half = rows // 2
    block = block_rows(size, cols)
    per = size // block

    def from_grad(d):
        return pl.BlockSpec((block, cols), lambda i, at: (at[d] // block + i, 0))

    piece = pl.BlockSpec((block, cols), lambda i, at: (i, 0))
    operands, in_specs = [], []
    if gots[0] is not None:
        operands += gots
        in_specs += [piece, piece]
    operands += [grad, grad]
    in_specs += [from_grad(0), from_grad(1)]
    out_shape = [jax.ShapeDtypeStruct((size, cols), BF16)] * 2
    out_specs = [piece, piece]
    aliases = {}
    if chunk is not None:
        whole = pl.BlockSpec((8, cols), lambda i, at: (0, 0))
        if state is not None:
            base = len(operands) + 1
            operands += state
            in_specs += [ANY, ANY, whole]
            aliases = {base: 2, base + 1: 3, base + 2: 4}
        out_shape += [
            jax.ShapeDtypeStruct((half, cols), BF16),
            jax.ShapeDtypeStruct((half, LANES), F32),
            jax.ShapeDtypeStruct((8, cols), F32),
        ]
        out_specs += [
            pl.BlockSpec((block, cols), lambda i, at: (chunk * per + i, 0)),
            pl.BlockSpec((block, LANES), lambda i, at: (chunk * per + i, 0)),
            whole,
        ]
    out = pl.pallas_call(
        functools.partial(sum_kernel, gots[0] is not None, chunk is not None, state is None),
        grid_spec=pltpu.PrefetchScalarGridSpec(
            num_scalar_prefetch=1, grid=(per,), in_specs=in_specs, out_specs=out_specs
        ),
        out_shape=out_shape,
        input_output_aliases=aliases,
        compiler_params=pltpu.CompilerParams(vmem_limit_bytes=16 * 1024 * 1024),
        cost_estimate=pl.CostEstimate(
            flops=4 * size * cols, bytes_accessed=12 * size * cols, transcendentals=0
        ),
        name="sum_step",
    )(at, *operands)
    return out[:2], list(out[2:])


def spread_kernel(size, chunk, with_got, with_out, sending, at_ref, *refs):
    refs = list(refs)
    gots = [refs.pop(0), refs.pop(0)] if with_got else [None, None]
    if chunk is not None:
        total_ref, row_ref, col_ref = refs.pop(0), refs.pop(0), refs.pop(0)
    if with_out:
        refs.pop(0)
    out_ref = refs.pop(0)
    sends = [refs.pop(0), refs.pop(0)] if sending else [None, None]
    update, sems = refs
    cols = update.shape[1]

    def copies(source, d):
        row = pl.multiple_of(at_ref[d], 16)
        keep = pltpu.make_async_copy(source, out_ref.at[pl.ds(row, size), :], sems.at[d, 0])
        give = pltpu.make_async_copy(source, sends[d], sems.at[d, 1]) if sending else None
        return keep, give

    for d in range(2):
        valid = at_ref[2 + d] == 1
        source = at_ref[4 + d] == 1
        if with_got:

            @pl.when(valid & jnp.logical_not(source))
            def _():
                keep, give = copies(gots[d], d)
                keep.start()
                if sending:
                    give.start()

        if chunk is not None:

            @pl.when(source)
            def _():
                for j in range(cols // LANES):
                    lanes = pl.ds(j * LANES, LANES)
                    wide = total_ref[:, lanes].astype(F32)
                    update[:, lanes] = (wide * row_ref[...] * col_ref[0:1, lanes]).astype(BF16)
                keep, give = copies(update, d)
                keep.start()
                if sending:
                    give.start()

    for d in range(2):

        @pl.when(at_ref[2 + d] == 1)
        def _():
            keep, give = copies(update, d)
            keep.wait()
            if sending:
                give.wait()


def spread_step(at, gots, parts, chunk, out, shape, size, sending):
    rows, cols = shape
    operands, in_specs, aliases = [], [], {}
    if gots[0] is not None:
        operands += gots
        in_specs += [ANY, ANY]
    if chunk is not None:
        operands += parts
        in_specs += [
            pl.BlockSpec((size, cols), lambda i, at: (chunk, 0)),
            pl.BlockSpec((size, LANES), lambda i, at: (chunk, 0)),
            pl.BlockSpec((8, cols), lambda i, at: (0, 0)),
        ]
    if out is not None:
        aliases = {len(operands) + 1: 0}
        operands.append(out)
        in_specs.append(ANY)
    out_shape = [jax.ShapeDtypeStruct(shape, BF16)]
    if sending:
        out_shape += [jax.ShapeDtypeStruct((size, cols), BF16)] * 2
    return pl.pallas_call(
        functools.partial(
            spread_kernel, size, chunk, gots[0] is not None, out is not None, sending
        ),
        grid_spec=pltpu.PrefetchScalarGridSpec(
            num_scalar_prefetch=1,
            grid=(1,),
            in_specs=in_specs,
            out_specs=[ANY] * len(out_shape),
            scratch_shapes=[pltpu.VMEM((size, cols), BF16), pltpu.SemaphoreType.DMA((2, 2))],
        ),
        out_shape=out_shape,
        input_output_aliases=aliases,
        compiler_params=pltpu.CompilerParams(vmem_limit_bytes=16 * 1024 * 1024),
        cost_estimate=pl.CostEstimate(
            flops=2 * size * cols, bytes_accessed=12 * size * cols, transcendentals=0
        ),
        name="spread_step",
    )(at, *operands)


def make_local(axis_sizes):
    n_dp, n_row, n_col = axis_sizes["dp"], axis_sizes["row"], axis_sizes["col"]
    last = n_dp - 1

    def spread_ends(value):
        total = value
        for j in range(1, n_dp):
            pairs = [[(0, j)], [(last, last - j)]]
            if j != last - j:
                pairs = [pairs[0] + pairs[1]]
            for some in pairs:
                total = total + lax.ppermute(value, "dp", some)
        return total

    def butterfly(value, axis, distance):
        n = axis_sizes[axis]
        return value + lax.ppermute(value, axis, [(i, i ^ distance) for i in range(n)])

    def distances(axis):
        out, d = [], 1
        while d < axis_sizes[axis]:
            out.append(d)
            d *= 2
        return out

    def local(grad_wi, grad_wo, row_wi, col_wi, row_wo, col_wo):
        place = lax.axis_index("dp")
        grads = (grad_wi[0], grad_wo[0])
        prevs = ((row_wi, col_wi), (row_wo, col_wo))
        shapes = [g.shape for g in grads]
        counts = [chunk_count(rows) for rows, _ in shapes]
        sizes = [rows // 2 // count for (rows, _), count in zip(shapes, counts)]

        position = jnp.stack([place, last - place])
        at_end = (place == last) | (place == 0)

        segments = []
        start = 0
        for kind in ("sum", "spread"):
            for m in range(2):
                segments.append((kind, m, start))
                start += counts[m]
        steps = start + LAG * last

        def hop(value, direction, senders):
            pairs = []
            for p in senders:
                if p < last:
                    pairs.append((p, p + 1) if direction == 0 else (last - p, last - p - 1))
            return lax.ppermute(value, "dp", pairs)

        states = {}
        finished = [0, 0]
        scales = {}
        results = {}
        cell = [None]

        def settle(value):
            value, _ = lax.optimization_barrier((value, cell[0]))
            return value

        def statistics(m):
            rows, cols = shapes[m]
            half = rows // 2
            while finished[m] < counts[m]:
                yield [], 1
            total, row_lanes, col_rows = states[m]
            row_part = jnp.sum(row_lanes, axis=1)
            col_part = jnp.sum(col_rows, axis=0)
            levels = max(len(distances("row")), len(distances("col")))
            for level in range(levels):
                if level < len(distances("col")):
                    row_part = butterfly(row_part, "col", distances("col")[level])
                if level < len(distances("row")):
                    col_part = butterfly(col_part, "row", distances("row")[level])
                yield [], 1
                row_part, col_part = settle((row_part, col_part))
            packed = jnp.concatenate(
                [
                    jnp.where(place == last, row_part, 0.0),
                    jnp.where(place == 0, row_part, 0.0),
                    jnp.where(at_end, col_part, 0.0),
                ]
            )
            packed = spread_ends(packed)
            yield [], FAR
            packed = settle(packed)
            row_new = BETA * prevs[m][0] + (1.0 - BETA) * (packed[:rows] / (cols * n_col))
            col_new = BETA * prevs[m][1] + (1.0 - BETA) * (packed[rows:] / (rows * n_row))
            row_scale = lax.rsqrt(jnp.where(place == 0, row_new[half:], row_new[:half]))
            col_scale = lax.rsqrt(col_new)
            energy = None
            for g in range(GROUPS):
                low, high = g * half // GROUPS, (g + 1) * half // GROUPS
                wide = settle(total)[low:high].astype(F32)
                raw = wide * row_scale[low:high, None] * col_scale[None, :]
                part = jnp.sum(raw * raw)
                energy = part if energy is None else energy + part
                if g == GROUPS // 2 - 1:
                    yield [energy], 1
            energy = jnp.broadcast_to(energy, (8, LANES))
            for axis in ("col", "row"):
                for distance in distances(axis):
                    energy = butterfly(energy, axis, distance)
                    yield [], 1
                    energy = settle(energy)
            energy = energy + lax.ppermute(energy, "dp", [(0, last), (last, 0)])
            yield [], FAR
            energy = settle(energy)[0, 0]
            rms = jnp.sqrt(energy / (rows * n_row * cols * n_col))
            row_final = row_scale / jnp.maximum(1.0, rms)
            scales[m] = [
                total,
                jnp.broadcast_to(row_final[:, None], (half, LANES)),
                jnp.broadcast_to(col_scale[None, :], (8, cols)),
            ]
            results[m] = (row_new, col_new)
            yield [scales[m][1], scales[m][2]], 1

        workers = [statistics(0), statistics(1)]
        wakes = [0, 0]

        def advance(m):
            try:
                return next(workers[m])
            except StopIteration:
                return [], steps

        outs = [None, None]
        inflight = {}
        arrived = {}
        tied = []
        for s in range(steps):
            before, tied = tied, []
            batch = []
            for index, (kind, m, begin) in enumerate(segments):
                members = [p for p in range(n_dp) if 0 <= s - LAG * p - begin < counts[m]]
                if not members:
                    continue
                while kind == "spread" and m not in scales:
                    advance(m)
                    wakes[m] = steps
                size = sizes[m]
                half = shapes[m][0] // 2
                gots = [inflight.pop((index, d, s - LAG), None) for d in range(2)]
                sending = min(members) < last
                number = s - begin - LAG * position
                at = jnp.clip(number, 0, counts[m] - 1) * size
                if kind == "sum":
                    at = jnp.concatenate([at + jnp.array([0, half]), place[None]])
                    chunk = s - begin - LAG * last if last in members else None
                    values, state = sum_step(
                        at.astype(jnp.int32), gots, grads[m], size, chunk, counts[m], states.get(m)
                    )
                    if chunk is not None:
                        states[m] = state
                        finished[m] += 1
                else:
                    valid = (number >= 0) & (number < counts[m])
                    source = valid & (position == 0)
                    at = jnp.concatenate([at + jnp.array([half, 0]), valid, source])
                    chunk = s - begin if 0 in members else None
                    outs[m], *values = spread_step(
                        at.astype(jnp.int32),
                        gots,
                        scales[m],
                        chunk,
                        outs[m],
                        shapes[m],
                        size,
                        sending,
                    )
                if sending:
                    for d in range(2):
                        batch.append((index, d, members, values[d]))
            if batch:
                values, _ = lax.optimization_barrier(
                    ([b[3] for b in batch], (before, arrived.get(s - LAG, [])))
                )
                tied = list(values)
            arrived[s] = []
            for (index, d, members, _), value in zip(batch, tied):
                inflight[index, d, s] = hop(value, d, members)
                arrived[s].append(inflight[index, d, s])
            cell[0] = list(tied)
            for m in range(2):
                if s >= wakes[m]:
                    ties, wait = advance(m)
                    tied = tied + ties
                    wakes[m] = s + wait
        return (outs[0], *results[0], outs[1], *results[1])

    return local


def solution(mesh):
    return jax.shard_map(
        make_local(dict(mesh.shape)),
        mesh=mesh,
        in_specs=(
            P("dp", "row", "col"),
            P("dp", "row", "col"),
            P("row"),
            P("col"),
            P("row"),
            P("col"),
        ),
        out_specs=(P("row", "col"), P("row"), P("col"), P("row", "col"), P("row"), P("col")),
        check_vma=False,
    )
```

```python
import functools

import jax
import jax.numpy as jnp
from jax import lax
from jax.experimental import pallas as pl
from jax.experimental.pallas import tpu as pltpu
from jax.sharding import PartitionSpec as P

BETA = 0.8
EPS_SQUARE = 1e-30
CHUNKS = 16
LAG = 2
GROUPS = 4
FAR = 2
LANES = 128
VMEM_BYTES = 48 * 1024 * 1024

F32 = jnp.float32
BF16 = jnp.bfloat16
ANY = pl.BlockSpec(memory_space=pl.ANY)


def chunk_count(rows):
    half = rows // 2
    count = CHUNKS
    while half % count or (half // count) % 16:
        count //= 2
    return count


def block_rows(size, cols):
    rows = size
    while rows % 32 == 0 and rows * cols > 16 * 8192:
        rows //= 2
    return rows


def sum_kernel(with_got, with_total, first_total, place_ref, *refs):
    refs = list(refs)
    gots = [refs.pop(0), refs.pop(0)] if with_got else [None, None]
    owns = [refs.pop(0), refs.pop(0)]
    if with_total and not first_total:
        refs.pop(0)
        refs.pop(0)
        col_in = refs.pop(0)
    sends = [refs.pop(0), refs.pop(0)]
    rows, cols = sends[0].shape
    low_end = place_ref[0] == 0
    if with_total:
        total_ref, row_ref, col_ref = refs

        @pl.when(pl.program_id(0) == 0)
        def _():
            col_ref[...] = jnp.zeros(col_ref.shape, F32) if first_total else col_in[...]

    row_part = jnp.zeros((rows, LANES), F32)
    for j in range(cols // LANES):
        lanes = pl.ds(j * LANES, LANES)
        values = []
        for got, own, send in zip(gots, owns, sends):
            value = own[:, lanes]
            if got is not None:
                value = (got[:, lanes].astype(F32) + value.astype(F32)).astype(BF16)
            send[:, lanes] = value
            values.append(value)
        if with_total:
            total = jnp.where(low_end, values[1], values[0])
            total_ref[:, lanes] = total
            wide = total.astype(F32)
            square = wide * wide + EPS_SQUARE
            row_part = row_part + square
            col_part = square[0:8]
            for r in range(8, rows, 8):
                col_part = col_part + square[r : r + 8]
            col_ref[:, lanes] += col_part
    if with_total:
        row_ref[...] = row_part


def number_of(place, d, turn, last):
    return turn - LAG * (place if d == 0 else last - place)


def sum_step(place, gots, grad, size, turn, count, last, chunk, state):
    rows, cols = grad.shape
    half = rows // 2
    block = block_rows(size, cols)
    per = size // block

    def from_grad(d):
        def index(i, at):
            number = jnp.clip(number_of(at[0], d, turn, last), 0, count - 1)
            return ((d * count + number) * per + i, 0)

        return pl.BlockSpec((block, cols), index)

    piece = pl.BlockSpec((block, cols), lambda i, at: (i, 0))
    operands, in_specs = [], []
    if gots[0] is not None:
        operands += gots
        in_specs += [piece, piece]
    operands += [grad, grad]
    in_specs += [from_grad(0), from_grad(1)]
    out_shape = [jax.ShapeDtypeStruct((size, cols), BF16)] * 2
    out_specs = [piece, piece]
    aliases = {}
    if chunk is not None:
        whole = pl.BlockSpec((8, cols), lambda i, at: (0, 0))
        if state is not None:
            base = len(operands) + 1
            operands += state
            in_specs += [ANY, ANY, whole]
            aliases = {base: 2, base + 1: 3, base + 2: 4}
        out_shape += [
            jax.ShapeDtypeStruct((half, cols), BF16),
            jax.ShapeDtypeStruct((half, LANES), F32),
            jax.ShapeDtypeStruct((8, cols), F32),
        ]
        out_specs += [
            pl.BlockSpec((block, cols), lambda i, at: (chunk * per + i, 0)),
            pl.BlockSpec((block, LANES), lambda i, at: (chunk * per + i, 0)),
            whole,
        ]
    out = pl.pallas_call(
        functools.partial(sum_kernel, gots[0] is not None, chunk is not None, state is None),
        grid_spec=pltpu.PrefetchScalarGridSpec(
            num_scalar_prefetch=1, grid=(per,), in_specs=in_specs, out_specs=out_specs
        ),
        out_shape=out_shape,
        input_output_aliases=aliases,
        compiler_params=pltpu.CompilerParams(vmem_limit_bytes=VMEM_BYTES),
        cost_estimate=pl.CostEstimate(
            flops=4 * size * cols, bytes_accessed=12 * size * cols, transcendentals=0
        ),
        name="sum_step",
    )(place, *operands)
    return out[:2], list(out[2:])


def spread_kernel(turn, count, last, chunk, with_got, with_out, sending, place_ref, *refs):
    refs = list(refs)
    gots = [refs.pop(0), refs.pop(0)] if with_got else [None, None]
    if chunk is not None:
        total_ref, row_ref, col_ref = refs.pop(0), refs.pop(0), refs.pop(0)
    if with_out:
        refs.pop(0)
    out_ref = refs.pop(0)
    sends = [refs.pop(0), refs.pop(0)] if sending else [None, None]
    update, sems = refs
    size, cols = update.shape
    numbers = [number_of(place_ref[0], d, turn, last) for d in range(2)]
    valids = [(number >= 0) & (number < count) for number in numbers]
    sources = [valids[0] & (place_ref[0] == 0), valids[1] & (place_ref[0] == last)]

    def copies(source, d):
        row = pl.multiple_of(((1 - d) * count + jnp.clip(numbers[d], 0, count - 1)) * size, 16)
        keep = pltpu.make_async_copy(source, out_ref.at[pl.ds(row, size), :], sems.at[d, 0])
        give = pltpu.make_async_copy(source, sends[d], sems.at[d, 1]) if sending else None
        return keep, give

    for d in range(2):
        if with_got:

            @pl.when(valids[d] & jnp.logical_not(sources[d]))
            def _():
                keep, give = copies(gots[d], d)
                keep.start()
                if sending:
                    give.start()

        if chunk is not None:

            @pl.when(sources[d])
            def _():
                for j in range(cols // LANES):
                    lanes = pl.ds(j * LANES, LANES)
                    wide = total_ref[:, lanes].astype(F32)
                    update[:, lanes] = (wide * row_ref[...] * col_ref[0:1, lanes]).astype(BF16)
                keep, give = copies(update, d)
                keep.start()
                if sending:
                    give.start()

    for d in range(2):

        @pl.when(valids[d])
        def _():
            keep, give = copies(update, d)
            keep.wait()
            if sending:
                give.wait()


def spread_step(place, gots, parts, size, turn, count, last, chunk, out, shape, sending):
    rows, cols = shape
    operands, in_specs, aliases = [], [], {}
    if gots[0] is not None:
        operands += gots
        in_specs += [ANY, ANY]
    if chunk is not None:
        operands += parts
        in_specs += [
            pl.BlockSpec((size, cols), lambda i, at: (chunk, 0)),
            pl.BlockSpec((size, LANES), lambda i, at: (chunk, 0)),
            pl.BlockSpec((8, cols), lambda i, at: (0, 0)),
        ]
    if out is not None:
        aliases = {len(operands) + 1: 0}
        operands.append(out)
        in_specs.append(ANY)
    out_shape = [jax.ShapeDtypeStruct(shape, BF16)]
    if sending:
        out_shape += [jax.ShapeDtypeStruct((size, cols), BF16)] * 2
    return pl.pallas_call(
        functools.partial(
            spread_kernel, turn, count, last, chunk, gots[0] is not None, out is not None, sending
        ),
        grid_spec=pltpu.PrefetchScalarGridSpec(
            num_scalar_prefetch=1,
            grid=(1,),
            in_specs=in_specs,
            out_specs=[ANY] * len(out_shape),
            scratch_shapes=[pltpu.VMEM((size, cols), BF16), pltpu.SemaphoreType.DMA((2, 2))],
        ),
        out_shape=out_shape,
        input_output_aliases=aliases,
        compiler_params=pltpu.CompilerParams(vmem_limit_bytes=VMEM_BYTES),
        cost_estimate=pl.CostEstimate(
            flops=2 * size * cols, bytes_accessed=12 * size * cols, transcendentals=0
        ),
        name="spread_step",
    )(place, *operands)


def make_local(axis_sizes):
    n_dp, n_row, n_col = axis_sizes["dp"], axis_sizes["row"], axis_sizes["col"]
    last = n_dp - 1

    def spread_ends(value):
        total = value
        for j in range(1, n_dp):
            pairs = [[(0, j)], [(last, last - j)]]
            if j != last - j:
                pairs = [pairs[0] + pairs[1]]
            for some in pairs:
                total = total + lax.ppermute(value, "dp", some)
        return total

    def butterfly(value, axis, distance):
        n = axis_sizes[axis]
        return value + lax.ppermute(value, axis, [(i, i ^ distance) for i in range(n)])

    def distances(axis):
        out, d = [], 1
        while d < axis_sizes[axis]:
            out.append(d)
            d *= 2
        return out

    def local(grad_wi, grad_wo, row_wi, col_wi, row_wo, col_wo):
        place = lax.axis_index("dp")
        grads = (grad_wi[0], grad_wo[0])
        prevs = ((row_wi, col_wi), (row_wo, col_wo))
        shapes = [g.shape for g in grads]
        counts = [chunk_count(rows) for rows, _ in shapes]
        sizes = [rows // 2 // count for (rows, _), count in zip(shapes, counts)]

        here = place[None].astype(jnp.int32)
        at_end = (place == last) | (place == 0)

        segments = []
        start = 0
        for kind in ("sum", "spread"):
            for m in range(2):
                segments.append((kind, m, start))
                start += counts[m]
        steps = start + LAG * last

        def hop(value, direction, senders):
            pairs = []
            for p in senders:
                if p < last:
                    pairs.append((p, p + 1) if direction == 0 else (last - p, last - p - 1))
            return lax.ppermute(value, "dp", pairs)

        states = {}
        finished = [0, 0]
        scales = {}
        results = {}
        cell = [None]

        def settle(value):
            value, _ = lax.optimization_barrier((value, cell[0]))
            return value

        def statistics(m):
            rows, cols = shapes[m]
            half = rows // 2
            while finished[m] < counts[m]:
                yield [], 1
            total, row_lanes, col_rows = states[m]
            row_part = jnp.sum(row_lanes, axis=1)
            col_part = jnp.sum(col_rows, axis=0)
            levels = max(len(distances("row")), len(distances("col")))
            for level in range(levels):
                if level < len(distances("col")):
                    row_part = butterfly(row_part, "col", distances("col")[level])
                if level < len(distances("row")):
                    col_part = butterfly(col_part, "row", distances("row")[level])
                yield [], 1
                row_part, col_part = settle((row_part, col_part))
            packed = jnp.concatenate(
                [
                    jnp.where(place == last, row_part, 0.0),
                    jnp.where(place == 0, row_part, 0.0),
                    jnp.where(at_end, col_part, 0.0),
                ]
            )
            packed = spread_ends(packed)
            yield [], FAR
            packed = settle(packed)
            row_new = BETA * prevs[m][0] + (1.0 - BETA) * (packed[:rows] / (cols * n_col))
            col_new = BETA * prevs[m][1] + (1.0 - BETA) * (packed[rows:] / (rows * n_row))
            row_scale = lax.rsqrt(jnp.where(place == 0, row_new[half:], row_new[:half]))
            col_scale = lax.rsqrt(col_new)
            energy = None
            for g in range(GROUPS):
                low, high = g * half // GROUPS, (g + 1) * half // GROUPS
                wide = settle(total)[low:high].astype(F32)
                raw = wide * row_scale[low:high, None] * col_scale[None, :]
                part = jnp.sum(raw * raw)
                energy = part if energy is None else energy + part
                if g == GROUPS // 2 - 1:
                    yield [energy], 1
            energy = jnp.broadcast_to(energy, (8, LANES))
            for axis in ("col", "row"):
                for distance in distances(axis):
                    energy = butterfly(energy, axis, distance)
                    yield [], 1
                    energy = settle(energy)
            energy = energy + lax.ppermute(energy, "dp", [(0, last), (last, 0)])
            yield [], FAR
            energy = settle(energy)[0, 0]
            rms = jnp.sqrt(energy / (rows * n_row * cols * n_col))
            row_final = row_scale / jnp.maximum(1.0, rms)
            scales[m] = [
                total,
                jnp.broadcast_to(row_final[:, None], (half, LANES)),
                jnp.broadcast_to(col_scale[None, :], (8, cols)),
            ]
            results[m] = (row_new, col_new)
            yield [scales[m][1], scales[m][2]], 1

        workers = [statistics(0), statistics(1)]
        wakes = [0, 0]

        def advance(m):
            try:
                return next(workers[m])
            except StopIteration:
                return [], steps

        outs = [None, None]
        inflight = {}
        arrived = {}
        tied = []
        for s in range(steps):
            before, tied = tied, []
            batch = []
            for index, (kind, m, begin) in enumerate(segments):
                members = [p for p in range(n_dp) if 0 <= s - LAG * p - begin < counts[m]]
                if not members:
                    continue
                while kind == "spread" and m not in scales:
                    advance(m)
                    wakes[m] = steps
                size = sizes[m]
                gots = [inflight.pop((index, d, s - LAG), None) for d in range(2)]
                sending = min(members) < last
                turn = s - begin
                if kind == "sum":
                    chunk = turn - LAG * last if last in members else None
                    values, state = sum_step(
                        here, gots, grads[m], size, turn, counts[m], last, chunk, states.get(m)
                    )
                    if chunk is not None:
                        states[m] = state
                        finished[m] += 1
                else:
                    chunk = turn if 0 in members else None
                    outs[m], *values = spread_step(
                        here,
                        gots,
                        scales[m],
                        size,
                        turn,
                        counts[m],
                        last,
                        chunk,
                        outs[m],
                        shapes[m],
                        sending,
                    )
                if sending:
                    for d in range(2):
                        batch.append((index, d, members, values[d]))
            if batch:
                values, _ = lax.optimization_barrier(
                    ([b[3] for b in batch], (before, arrived.get(s - LAG, [])))
                )
                tied = list(values)
            arrived[s] = []
            for (index, d, members, _), value in zip(batch, tied):
                inflight[index, d, s] = hop(value, d, members)
                arrived[s].append(inflight[index, d, s])
            cell[0] = list(tied)
            for m in range(2):
                if s >= wakes[m]:
                    ties, wait = advance(m)
                    tied = tied + ties
                    wakes[m] = s + wait
        return (outs[0], *results[0], outs[1], *results[1])

    return local


def solution(mesh):
    return jax.shard_map(
        make_local(dict(mesh.shape)),
        mesh=mesh,
        in_specs=(
            P("dp", "row", "col"),
            P("dp", "row", "col"),
            P("row"),
            P("col"),
            P("row"),
            P("col"),
        ),
        out_specs=(P("row", "col"), P("row"), P("col"), P("row", "col"), P("row"), P("col")),
        check_vma=False,
    )
```

```python
import functools

import jax
import jax.numpy as jnp
from jax import lax
from jax.experimental import pallas as pl
from jax.experimental.pallas import tpu as pltpu
from jax.sharding import PartitionSpec as P

BETA = 0.8
EPS_SQUARE = 1e-30
CHUNKS = 16
LAG = 2
GROUPS = 4
FAR = 2
LANES = 128
VMEM_BYTES = 48 * 1024 * 1024

F32 = jnp.float32
BF16 = jnp.bfloat16
ANY = pl.BlockSpec(memory_space=pl.ANY)


def chunk_count(shapes):
    count = CHUNKS
    while any(rows % (32 * count) for rows, _ in shapes):
        count //= 2
    return count


def step_kernel(plan, place_ref, *refs):
    refs = list(refs)
    gots = [refs.pop(0), refs.pop(0)] if plan["with_got"] else [None, None]
    taken = []
    for part in plan["parts"]:
        taken.append([refs.pop(0) for _ in range(part["operands"])])
    sends = [refs.pop(0), refs.pop(0)] if plan["sending"] else [None, None]
    given = []
    for part in plan["parts"]:
        given.append([refs.pop(0) for _ in range(part["results"])])
    (sems,) = refs

    place, last, count = place_ref[0], plan["last"], plan["count"]
    numbers = [plan["step"] - LAG * place, plan["step"] - LAG * (last - place)]
    positions = [place, last - place]

    def pieces(size, q, width):
        for j in range(q):
            for lane in range(0, width, LANES):
                yield pl.ds(j * size, size), pl.ds(lane, LANES), pl.ds(j * width + lane, LANES)

    for part, ins, outs in zip(plan["parts"], taken, given):
        size, q, width, begin = part["size"], part["q"], part["width"], part["begin"]
        here = [n - begin for n in numbers]
        valids = [(n >= 0) & (n < count) for n in here]
        if part["kind"] == "sum":
            for d in range(2):

                @pl.when(valids[d])
                def _():
                    for at, lanes, full in pieces(size, q, width):
                        value = ins[d][:, full]
                        if plan["with_got"]:
                            value = (gots[d][at, lanes].astype(F32) + value.astype(F32)).astype(BF16)
                        sends[d][at, lanes] = value

            if part["chunk"] is not None:
                total_ref, row_ref, col_ref = outs
                for d, end in ((0, last), (1, 0)):

                    @pl.when(place == end)
                    def _():
                        row_part = jnp.zeros((size, LANES), F32)
                        for at, lanes, full in pieces(size, q, width):
                            total = sends[d][at, lanes]
                            total_ref[:, full] = total
                            wide = total.astype(F32)
                            square = wide * wide + EPS_SQUARE
                            row_part = row_part + square
                            col_part = square[0:8]
                            for r in range(8, size, 8):
                                col_part = col_part + square[r : r + 8]
                            if not part["first"]:
                                col_part = col_part + ins[-1][:, full]
                            col_ref[:, full] = col_part
                        row_ref[...] = row_part

        else:
            out_ref = outs[0]

            def keep(source, d, j):
                row = ((1 - d) * count + jnp.clip(here[d], 0, count - 1)) * size
                return pltpu.make_async_copy(
                    source.at[pl.ds(j * size, size), :],
                    out_ref.at[pl.ds(pl.multiple_of(row, 16), size), pl.ds(j * width, width)],
                    sems.at[d, j],
                )

            for d in range(2):
                if part["chunk"] is not None:
                    total_ref, row_ref, col_ref = ins[:3]

                    @pl.when(valids[d] & (positions[d] == 0))
                    def _():
                        for at, lanes, full in pieces(size, q, width):
                            wide = total_ref[:, full].astype(F32)
                            update = wide * row_ref[...] * col_ref[0:1, full]
                            sends[d][at, lanes] = update.astype(BF16)
                        for j in range(q):
                            keep(sends[d], d, j).start()

                if plan["with_got"]:

                    @pl.when(valids[d] & (positions[d] > 0))
                    def _():
                        for j in range(q):
                            keep(gots[d], d, j).start()
                        if plan["sending"]:
                            for at, lanes, _ in pieces(size, q, width):
                                sends[d][at, lanes] = gots[d][at, lanes]

            for d in range(2):

                @pl.when(valids[d])
                def _():
                    for j in range(q):
                        keep(gots[d] if sends[d] is None else sends[d], d, j).wait()


def run_step(place, s, count, last, gots, parts, message, sending):
    window = pl.BlockSpec(message, lambda i, at: (0, 0))
    operands, in_specs, out_shape, out_specs, aliases = [], [], [], [], {}
    with_got = gots is not None
    if with_got:
        operands += gots
        in_specs += [window, window]
    if sending:
        out_shape += [jax.ShapeDtypeStruct(message, BF16)] * 2
        out_specs += [window, window]
    plans = []
    widest = 1
    for part in parts:
        rows, cols = part["shape"]
        half, size = rows // 2, rows // 2 // count
        q, width = cols // message[1], message[1]
        widest = max(widest, q)
        chunk = part["chunk"]
        block = pl.BlockSpec((size, cols), lambda i, at, k=chunk: (k, 0))
        lanes = pl.BlockSpec((size, LANES), lambda i, at, k=chunk: (k, 0))
        whole = pl.BlockSpec((8, cols), lambda i, at: (0, 0))
        before, results_before = len(operands), len(out_shape)
        if part["kind"] == "sum":
            for d in range(2):

                def from_grad(i, at, d=d, begin=part["begin"]):
                    number = s - begin - LAG * (at[0] if d == 0 else last - at[0])
                    return (d * count + jnp.clip(number, 0, count - 1), 0)

                operands.append(part["grad"])
                in_specs.append(pl.BlockSpec((size, cols), from_grad))
            if chunk is not None:
                if part["state"] is not None:
                    for k in range(3):
                        aliases[len(operands) + 1 + k] = len(out_shape) + k
                    operands += part["state"]
                    in_specs += [ANY, ANY, whole]
                out_shape += [
                    jax.ShapeDtypeStruct((half, cols), BF16),
                    jax.ShapeDtypeStruct((half, LANES), F32),
                    jax.ShapeDtypeStruct((8, cols), F32),
                ]
                out_specs += [block, lanes, whole]
        else:
            if chunk is not None:
                operands += part["scales"]
                in_specs += [block, lanes, whole]
            if part["out"] is not None:
                aliases[len(operands) + 1] = len(out_shape)
                operands.append(part["out"])
                in_specs.append(ANY)
            out_shape.append(jax.ShapeDtypeStruct((rows, cols), BF16))
            out_specs.append(ANY)
        plans.append(
            dict(
                kind=part["kind"],
                begin=part["begin"],
                chunk=chunk,
                first=part.get("state") is None,
                size=size,
                q=q,
                width=width,
                operands=len(operands) - before,
                results=len(out_shape) - results_before,
            )
        )
    plan = dict(
        step=s, count=count, last=last, with_got=with_got, sending=sending, parts=plans
    )
    elements = message[0] * message[1]
    out = pl.pallas_call(
        functools.partial(step_kernel, plan),
        grid_spec=pltpu.PrefetchScalarGridSpec(
            num_scalar_prefetch=1,
            grid=(1,),
            in_specs=in_specs,
            out_specs=out_specs,
            scratch_shapes=[pltpu.SemaphoreType.DMA((2, widest))],
        ),
        out_shape=out_shape,
        input_output_aliases=aliases,
        compiler_params=pltpu.CompilerParams(vmem_limit_bytes=VMEM_BYTES),
        cost_estimate=pl.CostEstimate(
            flops=4 * elements, bytes_accessed=12 * elements, transcendentals=0
        ),
        name="line_step",
    )(place, *operands)
    out = list(out)
    values = [out.pop(0), out.pop(0)] if sending else None
    return values, [[out.pop(0) for _ in range(plan["results"])] for plan in plans]


def make_local(axis_sizes):
    n_dp, n_row, n_col = axis_sizes["dp"], axis_sizes["row"], axis_sizes["col"]
    last = n_dp - 1

    def partner(value, axis, distance):
        n = axis_sizes[axis]
        return lax.ppermute(value, axis, [(i, i ^ distance) for i in range(n)])

    def distances(axis):
        out, d = [], 1
        while d < axis_sizes[axis]:
            out.append(d)
            d *= 2
        return out

    def local(grad_wi, grad_wo, row_wi, col_wi, row_wo, col_wo):
        place = lax.axis_index("dp")
        grads = (grad_wi[0], grad_wo[0])
        prevs = ((row_wi, col_wi), (row_wo, col_wo))
        shapes = [g.shape for g in grads]
        count = chunk_count(shapes)
        here = place[None].astype(jnp.int32)
        at_end = (place == last) | (place == 0)
        width = min(cols for _, cols in shapes)
        message = (shapes[0][0] * shapes[0][1] // (2 * count * width), width)

        kinds = [("sum", 0), ("sum", 1), ("spread", 0), ("spread", 1)]
        messages = len(kinds) * count
        steps = messages + LAG * last

        states = [None, None]
        finished = [0, 0]
        scales = {}
        results = {}
        cell = [None]

        def settle(value):
            value, _ = lax.optimization_barrier((value, cell[0]))
            return value

        def statistics(m):
            rows, cols = shapes[m]
            half = rows // 2
            while finished[m] < count:
                yield [], 1
            total, row_lanes, col_rows = states[m]
            row_part = jnp.sum(row_lanes, axis=1)
            col_part = jnp.sum(col_rows, axis=0)
            levels = max(len(distances("row")), len(distances("col")))
            for level in range(levels):
                row_other = col_other = None
                if level < len(distances("col")):
                    row_other = partner(row_part, "col", distances("col")[level])
                if level < len(distances("row")):
                    col_other = partner(col_part, "row", distances("row")[level])
                yield [], 1
                row_part, col_part, row_other, col_other = settle(
                    (row_part, col_part, row_other, col_other)
                )
                row_part = row_part if row_other is None else row_part + row_other
                col_part = col_part if col_other is None else col_part + col_other
            packed = jnp.concatenate(
                [
                    jnp.where(place == last, row_part, 0.0),
                    jnp.where(place == 0, row_part, 0.0),
                    jnp.where(at_end, col_part, 0.0),
                ]
            )
            far = lax.ppermute(packed, "dp", [(0, last), (last, 0)])
            yield [], FAR
            packed, far = settle((packed, far))

            def factors(sums):
                row_new = BETA * prevs[m][0] + (1.0 - BETA) * (sums[:rows] / (cols * n_col))
                col_new = BETA * prevs[m][1] + (1.0 - BETA) * (sums[rows:] / (rows * n_row))
                return row_new, col_new

            row_new, col_new = factors(packed + far)
            row_scale = lax.rsqrt(jnp.where(place == 0, row_new[half:], row_new[:half]))
            col_scale = lax.rsqrt(col_new)
            energy = None
            for g in range(GROUPS):
                low, high = g * half // GROUPS, (g + 1) * half // GROUPS
                wide = settle(total)[low:high].astype(F32)
                raw = wide * row_scale[low:high, None] * col_scale[None, :]
                part = jnp.sum(raw * raw)
                energy = part if energy is None else energy + part
                if g == GROUPS // 2 - 1:
                    yield [energy], 1
            energy = jnp.broadcast_to(energy, (8, LANES))
            for axis in ("col", "row"):
                for distance in distances(axis):
                    other = partner(energy, axis, distance)
                    yield [], 1
                    energy, other = settle((energy, other))
                    energy = energy + other
            other = lax.ppermute(energy, "dp", [(0, last), (last, 0)])
            yield [], FAR
            energy, other = settle((energy, other))
            energy = (energy + other)[0, 0]
            rms = jnp.sqrt(energy / (rows * n_row * cols * n_col))
            row_final = row_scale / jnp.maximum(1.0, rms)
            scales[m] = [
                total,
                jnp.broadcast_to(row_final[:, None], (half, LANES)),
                jnp.broadcast_to(col_scale[None, :], (8, cols)),
            ]
            yield [scales[m][1], scales[m][2]], count // 2
            sums = packed + far
            for j in range(1, last):
                for pairs in (
                    [[(0, j), (last, last - j)]] if j != last - j else [[(0, j)], [(last, j)]]
                ):
                    got = lax.ppermute(settle(packed), "dp", pairs)
                    yield [], FAR
                    sums = sums + settle(got)
            results[m] = factors(sums)
            yield list(results[m]), steps

        workers = [statistics(0), statistics(1)]
        wakes = [0, 0]
        outs = [None, None]
        inflight = {}
        tied = []
        for s in range(steps):
            before, tied = tied, []
            movers = [p for p in range(n_dp) if 0 <= s - LAG * p < messages]
            parts = []
            for index, (kind, m) in enumerate(kinds):
                begin = index * count
                members = [p for p in movers if begin <= s - LAG * p < begin + count]
                if not members:
                    continue
                part = dict(kind=kind, m=m, begin=begin, shape=shapes[m])
                if kind == "sum":
                    part["chunk"] = s - begin - LAG * last if last in members else None
                    part.update(grad=grads[m], state=states[m])
                else:
                    while m not in scales:
                        wakes[m] = s + next(workers[m])[1]
                    part["chunk"] = s - begin if 0 in members else None
                    part.update(scales=scales[m], out=outs[m])
                parts.append(part)
            gots = inflight.pop(s - LAG, None)
            sending = min(movers) < last
            values, given = run_step(here, s, count, last, gots, parts, message, sending)
            for part, made in zip(parts, given):
                if part["kind"] == "spread":
                    outs[part["m"]] = made[0]
                elif made:
                    states[part["m"]] = made
                    finished[part["m"]] += 1
            if sending:
                tied, _ = lax.optimization_barrier((values, (before, gots)))
                tied = list(tied)
                going = [p for p in movers if p < last]
                inflight[s] = [
                    lax.ppermute(tied[0], "dp", [(p, p + 1) for p in going]),
                    lax.ppermute(tied[1], "dp", [(last - p, last - p - 1) for p in going]),
                ]
                cell[0] = list(tied)
            for m in range(2):
                if s >= wakes[m]:
                    ties, wait = next(workers[m])
                    tied = tied + ties
                    wakes[m] = s + wait
        for m in range(2):
            while m not in results:
                next(workers[m])
        return (outs[0], *results[0], outs[1], *results[1])

    return local


def solution(mesh):
    return jax.shard_map(
        make_local(dict(mesh.shape)),
        mesh=mesh,
        in_specs=(
            P("dp", "row", "col"),
            P("dp", "row", "col"),
            P("row"),
            P("col"),
            P("row"),
            P("col"),
        ),
        out_specs=(P("row", "col"), P("row"), P("col"), P("row", "col"), P("row"), P("col")),
        check_vma=False,
    )
```

```python
import functools

import jax
import jax.numpy as jnp
from jax import lax
from jax.experimental import pallas as pl
from jax.experimental.pallas import tpu as pltpu
from jax.sharding import PartitionSpec as P

BETA = 0.8
EPS_SQUARE = 1e-30
CHUNKS = 16
LAG = 2
GROUPS = 4
FAR = 2
LANES = 128
VMEM_BYTES = 48 * 1024 * 1024

F32 = jnp.float32
BF16 = jnp.bfloat16
ANY = pl.BlockSpec(memory_space=pl.ANY)


def chunk_count(shapes):
    count = CHUNKS
    while any(rows % (32 * count) for rows, _ in shapes):
        count //= 2
    return count


def step_kernel(plan, place_ref, *refs):
    refs = list(refs)
    gots = [refs.pop(0), refs.pop(0)] if plan["with_got"] else [None, None]
    taken = []
    for part in plan["parts"]:
        taken.append([refs.pop(0) for _ in range(part["operands"])])
    sends = [refs.pop(0), refs.pop(0)] if plan["sending"] else [None, None]
    given = []
    for part in plan["parts"]:
        given.append([refs.pop(0) for _ in range(part["results"])])
    (sems,) = refs

    place, last, count = place_ref[0], plan["last"], plan["count"]
    numbers = [plan["step"] - LAG * place, plan["step"] - LAG * (last - place)]
    positions = [place, last - place]

    def pieces(size, q, width):
        for j in range(q):
            for lane in range(0, width, LANES):
                yield pl.ds(j * size, size), pl.ds(lane, LANES), pl.ds(j * width + lane, LANES)

    for part, ins, outs in zip(plan["parts"], taken, given):
        size, q, width, begin = part["size"], part["q"], part["width"], part["begin"]
        here = [n - begin for n in numbers]
        valids = [(n >= 0) & (n < count) for n in here]
        if part["kind"] == "sum":
            for d in range(2):

                @pl.when(valids[d])
                def _():
                    for at, lanes, full in pieces(size, q, width):
                        value = ins[d][:, full]
                        if plan["with_got"]:
                            value = (gots[d][at, lanes].astype(F32) + value.astype(F32)).astype(BF16)
                        sends[d][at, lanes] = value

            if part["chunk"] is not None:
                total_ref, row_ref, col_ref = outs
                for d, end in ((0, last), (1, 0)):

                    @pl.when(place == end)
                    def _():
                        row_part = jnp.zeros((size, LANES), F32)
                        for at, lanes, full in pieces(size, q, width):
                            total = sends[d][at, lanes]
                            total_ref[:, full] = total
                            wide = total.astype(F32)
                            square = wide * wide + EPS_SQUARE
                            row_part = row_part + square
                            col_part = square[0:8]
                            for r in range(8, size, 8):
                                col_part = col_part + square[r : r + 8]
                            if not part["first"]:
                                col_part = col_part + ins[-1][:, full]
                            col_ref[:, full] = col_part
                        row_ref[...] = row_part

        else:
            out_ref = outs[0]

            def keep(source, d, j):
                row = ((1 - d) * count + jnp.clip(here[d], 0, count - 1)) * size
                return pltpu.make_async_copy(
                    source.at[pl.ds(j * size, size), :],
                    out_ref.at[pl.ds(pl.multiple_of(row, 16), size), pl.ds(j * width, width)],
                    sems.at[d, j],
                )

            for d in range(2):
                if part["chunk"] is not None:
                    total_ref, row_ref, col_ref = ins[:3]

                    @pl.when(valids[d] & (positions[d] == 0))
                    def _():
                        for at, lanes, full in pieces(size, q, width):
                            wide = total_ref[:, full].astype(F32)
                            update = wide * row_ref[...] * col_ref[0:1, full]
                            sends[d][at, lanes] = update.astype(BF16)
                        for j in range(q):
                            keep(sends[d], d, j).start()

                if plan["with_got"]:

                    @pl.when(valids[d] & (positions[d] > 0))
                    def _():
                        for j in range(q):
                            keep(gots[d], d, j).start()
                        if plan["sending"]:
                            for at, lanes, _ in pieces(size, q, width):
                                sends[d][at, lanes] = gots[d][at, lanes]

            for d in range(2):

                @pl.when(valids[d])
                def _():
                    for j in range(q):
                        keep(gots[d] if sends[d] is None else sends[d], d, j).wait()


def run_step(place, s, count, last, gots, parts, message, sending):
    window = pl.BlockSpec(message, lambda i, at: (0, 0))
    operands, in_specs, out_shape, out_specs, aliases = [], [], [], [], {}
    with_got = gots is not None
    if with_got:
        operands += gots
        in_specs += [window, window]
    if sending:
        out_shape += [jax.ShapeDtypeStruct(message, BF16)] * 2
        out_specs += [window, window]
    plans = []
    widest = 1
    for part in parts:
        rows, cols = part["shape"]
        half, size = rows // 2, rows // 2 // count
        q, width = cols // message[1], message[1]
        widest = max(widest, q)
        chunk = part["chunk"]
        block = pl.BlockSpec((size, cols), lambda i, at, k=chunk: (k, 0))
        lanes = pl.BlockSpec((size, LANES), lambda i, at, k=chunk: (k, 0))
        whole = pl.BlockSpec((8, cols), lambda i, at: (0, 0))
        before, results_before = len(operands), len(out_shape)
        if part["kind"] == "sum":
            for d in range(2):

                def from_grad(i, at, d=d, begin=part["begin"]):
                    number = s - begin - LAG * (at[0] if d == 0 else last - at[0])
                    return (d * count + jnp.clip(number, 0, count - 1), 0)

                operands.append(part["grad"])
                in_specs.append(pl.BlockSpec((size, cols), from_grad))
            if chunk is not None:
                if part["state"] is not None:
                    for k in range(3):
                        aliases[len(operands) + 1 + k] = len(out_shape) + k
                    operands += part["state"]
                    in_specs += [ANY, ANY, whole]
                out_shape += [
                    jax.ShapeDtypeStruct((half, cols), BF16),
                    jax.ShapeDtypeStruct((half, LANES), F32),
                    jax.ShapeDtypeStruct((8, cols), F32),
                ]
                out_specs += [block, lanes, whole]
        else:
            if chunk is not None:
                operands += part["scales"]
                in_specs += [block, lanes, whole]
            if part["out"] is not None:
                aliases[len(operands) + 1] = len(out_shape)
                operands.append(part["out"])
                in_specs.append(ANY)
            out_shape.append(jax.ShapeDtypeStruct((rows, cols), BF16))
            out_specs.append(ANY)
        plans.append(
            dict(
                kind=part["kind"],
                begin=part["begin"],
                chunk=chunk,
                first=part.get("state") is None,
                size=size,
                q=q,
                width=width,
                operands=len(operands) - before,
                results=len(out_shape) - results_before,
            )
        )
    plan = dict(
        step=s, count=count, last=last, with_got=with_got, sending=sending, parts=plans
    )
    elements = message[0] * message[1]
    out = pl.pallas_call(
        functools.partial(step_kernel, plan),
        grid_spec=pltpu.PrefetchScalarGridSpec(
            num_scalar_prefetch=1,
            grid=(1,),
            in_specs=in_specs,
            out_specs=out_specs,
            scratch_shapes=[pltpu.SemaphoreType.DMA((2, widest))],
        ),
        out_shape=out_shape,
        input_output_aliases=aliases,
        compiler_params=pltpu.CompilerParams(vmem_limit_bytes=VMEM_BYTES),
        cost_estimate=pl.CostEstimate(
            flops=4 * elements, bytes_accessed=12 * elements, transcendentals=0
        ),
        name="line_step",
    )(place, *operands)
    out = list(out)
    values = [out.pop(0), out.pop(0)] if sending else None
    return values, [[out.pop(0) for _ in range(plan["results"])] for plan in plans]


def make_local(axis_sizes):
    n_dp, n_row, n_col = axis_sizes["dp"], axis_sizes["row"], axis_sizes["col"]
    last = n_dp - 1

    def partner(value, axis, distance):
        n = axis_sizes[axis]
        return lax.ppermute(value, axis, [(i, i ^ distance) for i in range(n)])

    def distances(axis):
        out, d = [], 1
        while d < axis_sizes[axis]:
            out.append(d)
            d *= 2
        return out

    def local(grad_wi, grad_wo, row_wi, col_wi, row_wo, col_wo):
        place = lax.axis_index("dp")
        grads = (grad_wi[0], grad_wo[0])
        prevs = ((row_wi, col_wi), (row_wo, col_wo))
        shapes = [g.shape for g in grads]
        count = chunk_count(shapes)
        here = place[None].astype(jnp.int32)
        at_end = (place == last) | (place == 0)
        width = min(cols for _, cols in shapes)
        message = (shapes[0][0] * shapes[0][1] // (2 * count * width), width)

        kinds = [("sum", 0), ("sum", 1), ("spread", 0), ("spread", 1)]
        messages = len(kinds) * count
        steps = messages + LAG * last

        states = [None, None]
        finished = [0, 0]
        scales = {}
        results = {}
        cell = [None]
        clock = [0]

        def settle(value):
            value, _ = lax.optimization_barrier((value, cell[0]))
            return value

        def statistics(m):
            rows, cols = shapes[m]
            half = rows // 2
            while finished[m] < count:
                yield [], 1
            total, row_lanes, col_rows = states[m]
            row_part = jnp.sum(row_lanes, axis=1)
            col_part = jnp.sum(col_rows, axis=0)
            levels = max(len(distances("row")), len(distances("col")))
            for level in range(levels):
                row_other = col_other = None
                if level < len(distances("col")):
                    row_other = partner(row_part, "col", distances("col")[level])
                if level < len(distances("row")):
                    col_other = partner(col_part, "row", distances("row")[level])
                yield [row_part, col_part], 1
                row_part, col_part, row_other, col_other = settle(
                    (row_part, col_part, row_other, col_other)
                )
                row_part = row_part if row_other is None else row_part + row_other
                col_part = col_part if col_other is None else col_part + col_other
            packed = jnp.concatenate(
                [
                    jnp.where(place == last, row_part, 0.0),
                    jnp.where(place == 0, row_part, 0.0),
                    jnp.where(at_end, col_part, 0.0),
                ]
            )
            far = lax.ppermute(packed, "dp", [(0, last), (last, 0)])
            yield [packed], FAR
            packed, far = settle((packed, far))

            def factors(sums):
                row_new = BETA * prevs[m][0] + (1.0 - BETA) * (sums[:rows] / (cols * n_col))
                col_new = BETA * prevs[m][1] + (1.0 - BETA) * (sums[rows:] / (rows * n_row))
                return row_new, col_new

            row_new, col_new = factors(packed + far)
            row_scale = lax.rsqrt(jnp.where(place == 0, row_new[half:], row_new[:half]))
            col_scale = lax.rsqrt(col_new)
            energy = None
            for g in range(GROUPS):
                low, high = g * half // GROUPS, (g + 1) * half // GROUPS
                wide = settle(total)[low:high].astype(F32)
                raw = wide * row_scale[low:high, None] * col_scale[None, :]
                part = jnp.sum(raw * raw)
                energy = part if energy is None else energy + part
                if g == GROUPS // 2 - 1:
                    yield [energy, row_scale, col_scale], 1
            energy = jnp.broadcast_to(energy, (8, LANES))
            for axis in ("col", "row"):
                for distance in distances(axis):
                    other = partner(energy, axis, distance)
                    yield [energy], 1
                    energy, other = settle((energy, other))
                    energy = energy + other
            other = lax.ppermute(energy, "dp", [(0, last), (last, 0)])
            yield [energy], FAR
            energy, other = settle((energy, other))
            energy = (energy + other)[0, 0]
            rms = jnp.sqrt(energy / (rows * n_row * cols * n_col))
            row_final = row_scale / jnp.maximum(1.0, rms)
            scales[m] = [
                total,
                jnp.broadcast_to(row_final[:, None], (half, LANES)),
                jnp.broadcast_to(col_scale[None, :], (8, cols)),
            ]
            yield [scales[m][1], scales[m][2]], max(1, 3 * count + 2 + 6 * m - clock[0])
            sums = packed + far
            for j in range(1, last):
                for pairs in (
                    [[(0, j), (last, last - j)]] if j != last - j else [[(0, j)], [(last, j)]]
                ):
                    got = lax.ppermute(settle(packed), "dp", pairs)
                    yield [sums], FAR
                    sums = sums + settle(got)
            results[m] = factors(sums)
            yield list(results[m]), steps

        workers = [statistics(0), statistics(1)]
        wakes = [0, 0]
        outs = [None, None]
        inflight = {}
        tied = []
        for s in range(steps):
            before, tied = tied, []
            clock[0] = s
            movers = [p for p in range(n_dp) if 0 <= s - LAG * p < messages]
            parts = []
            for index, (kind, m) in enumerate(kinds):
                begin = index * count
                members = [p for p in movers if begin <= s - LAG * p < begin + count]
                if not members:
                    continue
                part = dict(kind=kind, m=m, begin=begin, shape=shapes[m])
                if kind == "sum":
                    part["chunk"] = s - begin - LAG * last if last in members else None
                    part.update(grad=grads[m], state=states[m])
                else:
                    while m not in scales:
                        wakes[m] = s + next(workers[m])[1]
                    part["chunk"] = s - begin if 0 in members else None
                    part.update(scales=scales[m], out=outs[m])
                parts.append(part)
            gots = inflight.pop(s - LAG, None)
            sending = min(movers) < last
            values, given = run_step(here, s, count, last, gots, parts, message, sending)
            for part, made in zip(parts, given):
                if part["kind"] == "spread":
                    outs[part["m"]] = made[0]
                elif made:
                    states[part["m"]] = made
                    finished[part["m"]] += 1
            if sending:
                tied, _ = lax.optimization_barrier((values, (before, gots)))
                tied = list(tied)
                going = [p for p in movers if p < last]
                inflight[s] = [
                    lax.ppermute(tied[0], "dp", [(p, p + 1) for p in going]),
                    lax.ppermute(tied[1], "dp", [(last - p, last - p - 1) for p in going]),
                ]
                cell[0] = list(tied)
            for m in range(2):
                if s >= wakes[m]:
                    ties, wait = next(workers[m])
                    tied = tied + ties
                    wakes[m] = s + wait
        for m in range(2):
            while m not in results:
                next(workers[m])
        return (outs[0], *results[0], outs[1], *results[1])

    return local


def solution(mesh):
    return jax.shard_map(
        make_local(dict(mesh.shape)),
        mesh=mesh,
        in_specs=(
            P("dp", "row", "col"),
            P("dp", "row", "col"),
            P("row"),
            P("col"),
            P("row"),
            P("col"),
        ),
        out_specs=(P("row", "col"), P("row"), P("col"), P("row", "col"), P("row"), P("col")),
        check_vma=False,
    )
```

```python
import functools

import jax
import jax.numpy as jnp
from jax import lax
from jax.experimental import pallas as pl
from jax.experimental.pallas import tpu as pltpu
from jax.sharding import PartitionSpec as P

BETA = 0.8
EPS_SQUARE = 1e-30
CHUNKS = 16
LAG = 2
GROUPS = 4
FAR = 2
LANES = 128
VMEM_BYTES = 48 * 1024 * 1024

F32 = jnp.float32
BF16 = jnp.bfloat16
ANY = pl.BlockSpec(memory_space=pl.ANY)


def chunk_count(shapes):
    count = CHUNKS
    while any(rows % (32 * count) for rows, _ in shapes):
        count //= 2
    return count


def step_kernel(plan, place_ref, *refs):
    refs = list(refs)
    gots = [refs.pop(0), refs.pop(0)] if plan["with_got"] else [None, None]
    taken = []
    for part in plan["parts"]:
        taken.append([refs.pop(0) for _ in range(part["operands"])])
    sends = [refs.pop(0), refs.pop(0)] if plan["sending"] else [None, None]
    given = []
    for part in plan["parts"]:
        given.append([refs.pop(0) for _ in range(part["results"])])
    (sems,) = refs

    place, last, count = place_ref[0], plan["last"], plan["count"]
    numbers = [plan["step"] - LAG * place, plan["step"] - LAG * (last - place)]
    positions = [place, last - place]

    def pieces(size, q, width):
        for j in range(q):
            for lane in range(0, width, LANES):
                yield pl.ds(j * size, size), pl.ds(lane, LANES), pl.ds(j * width + lane, LANES)

    for part, ins, outs in zip(plan["parts"], taken, given):
        size, q, width, begin = part["size"], part["q"], part["width"], part["begin"]
        here = [n - begin for n in numbers]
        valids = [(n >= 0) & (n < count) for n in here]
        if part["kind"] == "sum":
            for d in range(2):

                @pl.when(valids[d])
                def _():
                    for at, lanes, full in pieces(size, q, width):
                        value = ins[d][:, full]
                        if plan["with_got"]:
                            value = (gots[d][at, lanes].astype(F32) + value.astype(F32)).astype(BF16)
                        sends[d][at, lanes] = value

            if part["chunk"] is not None:
                total_ref, row_ref, col_ref = outs
                for d, end in ((0, last), (1, 0)):

                    @pl.when(place == end)
                    def _():
                        row_part = jnp.zeros((size, LANES), F32)
                        for at, lanes, full in pieces(size, q, width):
                            total = sends[d][at, lanes]
                            total_ref[:, full] = total
                            wide = total.astype(F32)
                            square = wide * wide + EPS_SQUARE
                            row_part = row_part + square
                            col_part = square[0:8]
                            for r in range(8, size, 8):
                                col_part = col_part + square[r : r + 8]
                            if not part["first"]:
                                col_part = col_part + ins[-1][:, full]
                            col_ref[:, full] = col_part
                        row_ref[...] = row_part

        else:
            out_ref = outs[0]

            def keep(source, d, j):
                row = ((1 - d) * count + jnp.clip(here[d], 0, count - 1)) * size
                return pltpu.make_async_copy(
                    source.at[pl.ds(j * size, size), :],
                    out_ref.at[pl.ds(pl.multiple_of(row, 16), size), pl.ds(j * width, width)],
                    sems.at[d, j],
                )

            for d in range(2):
                if part["chunk"] is not None:
                    total_ref, row_ref, col_ref = ins[:3]

                    @pl.when(valids[d] & (positions[d] == 0))
                    def _():
                        for at, lanes, full in pieces(size, q, width):
                            wide = total_ref[:, full].astype(F32)
                            update = wide * row_ref[...] * col_ref[0:1, full]
                            sends[d][at, lanes] = update.astype(BF16)
                        for j in range(q):
                            keep(sends[d], d, j).start()

                if plan["with_got"]:

                    @pl.when(valids[d] & (positions[d] > 0))
                    def _():
                        for j in range(q):
                            keep(gots[d], d, j).start()
                        if plan["sending"]:
                            for at, lanes, _ in pieces(size, q, width):
                                sends[d][at, lanes] = gots[d][at, lanes]

            for d in range(2):

                @pl.when(valids[d])
                def _():
                    for j in range(q):
                        keep(gots[d] if sends[d] is None else sends[d], d, j).wait()


def run_step(place, s, count, last, gots, parts, message, sending):
    window = pl.BlockSpec(message, lambda i, at: (0, 0))
    operands, in_specs, out_shape, out_specs, aliases = [], [], [], [], {}
    with_got = gots is not None
    if with_got:
        operands += gots
        in_specs += [window, window]
    if sending:
        out_shape += [jax.ShapeDtypeStruct(message, BF16)] * 2
        out_specs += [window, window]
    plans = []
    widest = 1
    for part in parts:
        rows, cols = part["shape"]
        half, size = rows // 2, rows // 2 // count
        q, width = cols // message[1], message[1]
        widest = max(widest, q)
        chunk = part["chunk"]
        block = pl.BlockSpec((size, cols), lambda i, at, k=chunk: (k, 0))
        lanes = pl.BlockSpec((size, LANES), lambda i, at, k=chunk: (k, 0))
        whole = pl.BlockSpec((8, cols), lambda i, at: (0, 0))
        before, results_before = len(operands), len(out_shape)
        if part["kind"] == "sum":
            for d in range(2):

                def from_grad(i, at, d=d, begin=part["begin"]):
                    number = s - begin - LAG * (at[0] if d == 0 else last - at[0])
                    return (d * count + jnp.clip(number, 0, count - 1), 0)

                operands.append(part["grad"])
                in_specs.append(pl.BlockSpec((size, cols), from_grad))
            if chunk is not None:
                if part["state"] is not None:
                    for k in range(3):
                        aliases[len(operands) + 1 + k] = len(out_shape) + k
                    operands += part["state"]
                    in_specs += [ANY, ANY, whole]
                out_shape += [
                    jax.ShapeDtypeStruct((half, cols), BF16),
                    jax.ShapeDtypeStruct((half, LANES), F32),
                    jax.ShapeDtypeStruct((8, cols), F32),
                ]
                out_specs += [block, lanes, whole]
        else:
            if chunk is not None:
                operands += part["scales"]
                in_specs += [block, lanes, whole]
            if part["out"] is not None:
                aliases[len(operands) + 1] = len(out_shape)
                operands.append(part["out"])
                in_specs.append(ANY)
            out_shape.append(jax.ShapeDtypeStruct((rows, cols), BF16))
            out_specs.append(ANY)
        plans.append(
            dict(
                kind=part["kind"],
                begin=part["begin"],
                chunk=chunk,
                first=part.get("state") is None,
                size=size,
                q=q,
                width=width,
                operands=len(operands) - before,
                results=len(out_shape) - results_before,
            )
        )
    plan = dict(
        step=s, count=count, last=last, with_got=with_got, sending=sending, parts=plans
    )
    elements = message[0] * message[1]
    out = pl.pallas_call(
        functools.partial(step_kernel, plan),
        grid_spec=pltpu.PrefetchScalarGridSpec(
            num_scalar_prefetch=1,
            grid=(1,),
            in_specs=in_specs,
            out_specs=out_specs,
            scratch_shapes=[pltpu.SemaphoreType.DMA((2, widest))],
        ),
        out_shape=out_shape,
        input_output_aliases=aliases,
        compiler_params=pltpu.CompilerParams(vmem_limit_bytes=VMEM_BYTES),
        cost_estimate=pl.CostEstimate(
            flops=4 * elements, bytes_accessed=12 * elements, transcendentals=0
        ),
        name="line_step",
    )(place, *operands)
    out = list(out)
    values = [out.pop(0), out.pop(0)] if sending else None
    return values, [[out.pop(0) for _ in range(plan["results"])] for plan in plans]


def make_local(axis_sizes):
    n_dp, n_row, n_col = axis_sizes["dp"], axis_sizes["row"], axis_sizes["col"]
    last = n_dp - 1

    def partner(value, axis, distance):
        n = axis_sizes[axis]
        return lax.ppermute(value, axis, [(i, i ^ distance) for i in range(n)])

    def distances(axis):
        out, d = [], 1
        while d < axis_sizes[axis]:
            out.append(d)
            d *= 2
        return out

    def local(grad_wi, grad_wo, row_wi, col_wi, row_wo, col_wo):
        place = lax.axis_index("dp")
        grads = (grad_wi[0], grad_wo[0])
        prevs = ((row_wi, col_wi), (row_wo, col_wo))
        shapes = [g.shape for g in grads]
        count = chunk_count(shapes)
        here = place[None].astype(jnp.int32)
        at_end = (place == last) | (place == 0)
        width = min(cols for _, cols in shapes)
        message = (shapes[0][0] * shapes[0][1] // (2 * count * width), width)

        kinds = [("sum", 0), ("sum", 1), ("spread", 0), ("spread", 1)]
        messages = len(kinds) * count
        steps = messages + LAG * last

        states = [None, None]
        finished = [0, 0]
        scales = {}
        results = {}
        sums = {}
        cell = [None]

        def settle(value):
            value, _ = lax.optimization_barrier((value, cell[0]))
            return value

        def statistics(m):
            rows, cols = shapes[m]
            half = rows // 2
            while finished[m] < count:
                yield [], 1
            total, row_lanes, col_rows = states[m]
            row_part = jnp.sum(row_lanes, axis=1)
            col_part = jnp.sum(col_rows, axis=0)
            levels = max(len(distances("row")), len(distances("col")))
            for level in range(levels):
                row_other = col_other = None
                if level < len(distances("col")):
                    row_other = partner(row_part, "col", distances("col")[level])
                if level < len(distances("row")):
                    col_other = partner(col_part, "row", distances("row")[level])
                yield [row_part, col_part], 1
                row_part, col_part, row_other, col_other = settle(
                    (row_part, col_part, row_other, col_other)
                )
                row_part = row_part if row_other is None else row_part + row_other
                col_part = col_part if col_other is None else col_part + col_other
            packed = jnp.concatenate(
                [
                    jnp.where(place == last, row_part, 0.0),
                    jnp.where(place == 0, row_part, 0.0),
                    jnp.where(at_end, col_part, 0.0),
                ]
            )
            far = lax.ppermute(packed, "dp", [(0, last), (last, 0)])
            yield [packed], FAR
            packed, far = settle((packed, far))

            row_new, col_new = factors(m, packed + far)
            row_scale = lax.rsqrt(jnp.where(place == 0, row_new[half:], row_new[:half]))
            col_scale = lax.rsqrt(col_new)
            energy = None
            for g in range(GROUPS):
                low, high = g * half // GROUPS, (g + 1) * half // GROUPS
                wide = settle(total)[low:high].astype(F32)
                raw = wide * row_scale[low:high, None] * col_scale[None, :]
                part = jnp.sum(raw * raw)
                energy = part if energy is None else energy + part
            energy = jnp.broadcast_to(energy, (8, LANES))
            for axis in ("col", "row"):
                for distance in distances(axis):
                    other = partner(energy, axis, distance)
                    yield [energy], 1
                    energy, other = settle((energy, other))
                    energy = energy + other
            other = lax.ppermute(energy, "dp", [(0, last), (last, 0)])
            yield [energy], FAR + m
            energy, other = settle((energy, other))
            energy = (energy + other)[0, 0]
            rms = jnp.sqrt(energy / (rows * n_row * cols * n_col))
            row_final = row_scale / jnp.maximum(1.0, rms)
            scales[m] = [
                total,
                jnp.broadcast_to(row_final[:, None], (half, LANES)),
                jnp.broadcast_to(col_scale[None, :], (8, cols)),
            ]
            sums[m] = (packed, far)
            yield [scales[m][1], scales[m][2]], steps

        def factors(m, total):
            rows, cols = shapes[m]
            row_new = BETA * prevs[m][0] + (1.0 - BETA) * (total[:rows] / (cols * n_col))
            col_new = BETA * prevs[m][1] + (1.0 - BETA) * (total[rows:] / (rows * n_row))
            return row_new, col_new

        def closing():
            packed, far = (jnp.concatenate([sums[m][k] for m in range(2)]) for k in range(2))
            total = packed + far
            for j in range(1, last):
                for pairs in (
                    [[(0, j), (last, last - j)]] if j != last - j else [[(0, j)], [(last, j)]]
                ):
                    got = lax.ppermute(settle(packed), "dp", pairs)
                    yield [total], FAR
                    total = total + settle(got)
            cut = sum(shapes[0])
            results[0] = factors(0, total[:cut])
            results[1] = factors(1, total[cut:])
            yield [*results[0], *results[1]], steps

        workers = [statistics(0), statistics(1), closing()]
        wakes = [0, 0, messages - 2]
        outs = [None, None]
        inflight = {}
        tied = []
        for s in range(steps):
            before, tied = tied, []
            movers = [p for p in range(n_dp) if 0 <= s - LAG * p < messages]
            parts = []
            for index, (kind, m) in enumerate(kinds):
                begin = index * count
                members = [p for p in movers if begin <= s - LAG * p < begin + count]
                if not members:
                    continue
                part = dict(kind=kind, m=m, begin=begin, shape=shapes[m])
                if kind == "sum":
                    part["chunk"] = s - begin - LAG * last if last in members else None
                    part.update(grad=grads[m], state=states[m])
                else:
                    while m not in scales:
                        wakes[m] = s + next(workers[m])[1]
                    part["chunk"] = s - begin if 0 in members else None
                    part.update(scales=scales[m], out=outs[m])
                parts.append(part)
            gots = inflight.pop(s - LAG, None)
            sending = min(movers) < last
            values, given = run_step(here, s, count, last, gots, parts, message, sending)
            for part, made in zip(parts, given):
                if part["kind"] == "spread":
                    outs[part["m"]] = made[0]
                elif made:
                    states[part["m"]] = made
                    finished[part["m"]] += 1
            if sending:
                tied, _ = lax.optimization_barrier((values, (before, gots)))
                tied = list(tied)
                going = [p for p in movers if p < last]
                inflight[s] = [
                    lax.ppermute(tied[0], "dp", [(p, p + 1) for p in going]),
                    lax.ppermute(tied[1], "dp", [(last - p, last - p - 1) for p in going]),
                ]
                cell[0] = list(tied)
            for w, worker in enumerate(workers):
                if s >= wakes[w]:
                    ties, wait = next(worker)
                    tied = tied + ties
                    wakes[w] = s + wait
        while not results:
            next(workers[2])
        return (outs[0], *results[0], outs[1], *results[1])

    return local


def solution(mesh):
    return jax.shard_map(
        make_local(dict(mesh.shape)),
        mesh=mesh,
        in_specs=(
            P("dp", "row", "col"),
            P("dp", "row", "col"),
            P("row"),
            P("col"),
            P("row"),
            P("col"),
        ),
        out_specs=(P("row", "col"), P("row"), P("col"), P("row", "col"), P("row"), P("col")),
        check_vma=False,
    )
```

```python
import functools

import jax
import jax.numpy as jnp
from jax import lax
from jax.experimental import pallas as pl
from jax.experimental.pallas import tpu as pltpu
from jax.sharding import PartitionSpec as P

BETA = 0.8
EPS_SQUARE = 1e-30
CHUNKS = 16
LAG = 2
GROUPS = 4
FAR = 2
LANES = 128
PIECE = 16384
VMEM_BYTES = 48 * 1024 * 1024

F32 = jnp.float32
BF16 = jnp.bfloat16
ANY = pl.BlockSpec(memory_space=pl.ANY)


def chunk_count(shapes):
    count = CHUNKS
    while any(rows % (32 * count) for rows, _ in shapes):
        count //= 2
    return count


def step_kernel(plan, place_ref, *refs):
    refs = list(refs)
    gots = [refs.pop(0), refs.pop(0)] if plan["with_got"] else [None, None]
    taken = []
    for part in plan["parts"]:
        taken.append([refs.pop(0) for _ in range(part["operands"])])
    sends = [refs.pop(0), refs.pop(0)] if plan["sending"] else [None, None]
    given = []
    for part in plan["parts"]:
        given.append([refs.pop(0) for _ in range(part["results"])])
    (sems,) = refs

    place, last, count = place_ref[0], plan["last"], plan["count"]
    numbers = [plan["step"] - LAG * place, plan["step"] - LAG * (last - place)]
    positions = [place, last - place]

    def each_piece(size, q, width, body, carry=0):
        step = min(width, max(LANES, PIECE // size // LANES * LANES))
        across = width // step

        def turn(t, carry):
            at = pl.ds(pl.multiple_of(t // across * size, 16), size)
            lanes = pl.ds(pl.multiple_of(t % across * step, LANES), step)
            return body(at, lanes, pl.ds(pl.multiple_of(t * step, LANES), step), carry)

        return lax.fori_loop(0, q * across, turn, carry)

    for part, ins, outs in zip(plan["parts"], taken, given):
        size, q, width, begin = part["size"], part["q"], part["width"], part["begin"]
        here = [n - begin for n in numbers]
        valids = [(n >= 0) & (n < count) for n in here]
        if part["kind"] == "sum":
            for d in range(2):

                @pl.when(valids[d])
                def _():
                    def add(at, lanes, full, carry):
                        value = ins[d][:, full]
                        if plan["with_got"]:
                            value = (gots[d][at, lanes].astype(F32) + value.astype(F32)).astype(BF16)
                        sends[d][at, lanes] = value
                        return carry

                    each_piece(size, q, width, add)

            if part["chunk"] is not None:
                total_ref, row_ref, col_ref = outs
                for d, end in ((0, last), (1, 0)):

                    @pl.when(place == end)
                    def _():
                        def measure(at, lanes, full, row_part):
                            total = sends[d][at, lanes]
                            total_ref[:, full] = total
                            wide = total.astype(F32)
                            square = wide * wide + EPS_SQUARE
                            for lane in range(0, square.shape[1], LANES):
                                row_part = row_part + square[:, lane : lane + LANES]
                            col_part = square[0:8]
                            for r in range(8, size, 8):
                                col_part = col_part + square[r : r + 8]
                            if not part["first"]:
                                col_part = col_part + ins[-1][:, full]
                            col_ref[:, full] = col_part
                            return row_part

                        row_ref[...] = each_piece(
                            size, q, width, measure, jnp.zeros((size, LANES), F32)
                        )

        else:
            out_ref = outs[0]

            def keep(source, d, j):
                row = ((1 - d) * count + jnp.clip(here[d], 0, count - 1)) * size
                return pltpu.make_async_copy(
                    source.at[pl.ds(j * size, size), :],
                    out_ref.at[pl.ds(pl.multiple_of(row, 16), size), pl.ds(j * width, width)],
                    sems.at[d, j],
                )

            for d in range(2):
                if part["chunk"] is not None:
                    total_ref, row_ref, col_ref = ins[:3]

                    @pl.when(valids[d] & (positions[d] == 0))
                    def _():
                        def scale(at, lanes, full, carry):
                            wide = total_ref[:, full].astype(F32)
                            rows = jnp.concatenate([row_ref[...]] * (wide.shape[1] // LANES), axis=1)
                            update = wide * rows * col_ref[0:1, full]
                            sends[d][at, lanes] = update.astype(BF16)
                            return carry

                        each_piece(size, q, width, scale)
                        for j in range(q):
                            keep(sends[d], d, j).start()

                if plan["with_got"]:

                    @pl.when(valids[d] & (positions[d] > 0))
                    def _():
                        for j in range(q):
                            keep(gots[d], d, j).start()
                        if plan["sending"]:
                            def forward(at, lanes, full, carry):
                                sends[d][at, lanes] = gots[d][at, lanes]
                                return carry

                            each_piece(size, q, width, forward)

            for d in range(2):

                @pl.when(valids[d])
                def _():
                    for j in range(q):
                        keep(gots[d] if sends[d] is None else sends[d], d, j).wait()


def run_step(place, s, count, last, gots, parts, message, sending):
    window = pl.BlockSpec(message, lambda i, at: (0, 0))
    operands, in_specs, out_shape, out_specs, aliases = [], [], [], [], {}
    with_got = gots is not None
    if with_got:
        operands += gots
        in_specs += [window, window]
    if sending:
        out_shape += [jax.ShapeDtypeStruct(message, BF16)] * 2
        out_specs += [window, window]
    plans = []
    widest = 1
    for part in parts:
        rows, cols = part["shape"]
        half, size = rows // 2, rows // 2 // count
        q, width = cols // message[1], message[1]
        widest = max(widest, q)
        chunk = part["chunk"]
        block = pl.BlockSpec((size, cols), lambda i, at, k=chunk: (k, 0))
        lanes = pl.BlockSpec((size, LANES), lambda i, at, k=chunk: (k, 0))
        whole = pl.BlockSpec((8, cols), lambda i, at: (0, 0))
        before, results_before = len(operands), len(out_shape)
        if part["kind"] == "sum":
            for d in range(2):

                def from_grad(i, at, d=d, begin=part["begin"]):
                    number = s - begin - LAG * (at[0] if d == 0 else last - at[0])
                    return (d * count + jnp.clip(number, 0, count - 1), 0)

                operands.append(part["grad"])
                in_specs.append(pl.BlockSpec((size, cols), from_grad))
            if chunk is not None:
                if part["state"] is not None:
                    for k in range(3):
                        aliases[len(operands) + 1 + k] = len(out_shape) + k
                    operands += part["state"]
                    in_specs += [ANY, ANY, whole]
                out_shape += [
                    jax.ShapeDtypeStruct((half, cols), BF16),
                    jax.ShapeDtypeStruct((half, LANES), F32),
                    jax.ShapeDtypeStruct((8, cols), F32),
                ]
                out_specs += [block, lanes, whole]
        else:
            if chunk is not None:
                operands += part["scales"]
                in_specs += [block, lanes, whole]
            if part["out"] is not None:
                aliases[len(operands) + 1] = len(out_shape)
                operands.append(part["out"])
                in_specs.append(ANY)
            out_shape.append(jax.ShapeDtypeStruct((rows, cols), BF16))
            out_specs.append(ANY)
        plans.append(
            dict(
                kind=part["kind"],
                begin=part["begin"],
                chunk=chunk,
                first=part.get("state") is None,
                size=size,
                q=q,
                width=width,
                operands=len(operands) - before,
                results=len(out_shape) - results_before,
            )
        )
    plan = dict(
        step=s, count=count, last=last, with_got=with_got, sending=sending, parts=plans
    )
    elements = message[0] * message[1]
    out = pl.pallas_call(
        functools.partial(step_kernel, plan),
        grid_spec=pltpu.PrefetchScalarGridSpec(
            num_scalar_prefetch=1,
            grid=(1,),
            in_specs=in_specs,
            out_specs=out_specs,
            scratch_shapes=[pltpu.SemaphoreType.DMA((2, widest))],
        ),
        out_shape=out_shape,
        input_output_aliases=aliases,
        compiler_params=pltpu.CompilerParams(vmem_limit_bytes=VMEM_BYTES),
        cost_estimate=pl.CostEstimate(
            flops=4 * elements, bytes_accessed=12 * elements, transcendentals=0
        ),
        name="line_step",
    )(place, *operands)
    out = list(out)
    values = [out.pop(0), out.pop(0)] if sending else None
    return values, [[out.pop(0) for _ in range(plan["results"])] for plan in plans]


def make_local(axis_sizes):
    n_dp, n_row, n_col = axis_sizes["dp"], axis_sizes["row"], axis_sizes["col"]
    last = n_dp - 1

    def partner(value, axis, distance):
        n = axis_sizes[axis]
        return lax.ppermute(value, axis, [(i, i ^ distance) for i in range(n)])

    def distances(axis):
        out, d = [], 1
        while d < axis_sizes[axis]:
            out.append(d)
            d *= 2
        return out

    def local(grad_wi, grad_wo, row_wi, col_wi, row_wo, col_wo):
        place = lax.axis_index("dp")
        grads = (grad_wi[0], grad_wo[0])
        prevs = ((row_wi, col_wi), (row_wo, col_wo))
        shapes = [g.shape for g in grads]
        count = chunk_count(shapes)
        here = place[None].astype(jnp.int32)
        at_end = (place == last) | (place == 0)
        width = min(cols for _, cols in shapes)
        message = (shapes[0][0] * shapes[0][1] // (2 * count * width), width)

        kinds = [("sum", 0), ("sum", 1), ("spread", 0), ("spread", 1)]
        messages = len(kinds) * count
        steps = messages + LAG * last

        states = [None, None]
        finished = [0, 0]
        scales = {}
        results = {}
        sums = {}
        cell = [None]

        def settle(value):
            value, _ = lax.optimization_barrier((value, cell[0]))
            return value

        def statistics(m):
            rows, cols = shapes[m]
            half = rows // 2
            while finished[m] < count:
                yield [], 1
            total, row_lanes, col_rows = states[m]
            row_part = jnp.sum(row_lanes, axis=1)
            col_part = jnp.sum(col_rows, axis=0)
            levels = max(len(distances("row")), len(distances("col")))
            for level in range(levels):
                row_other = col_other = None
                if level < len(distances("col")):
                    row_other = partner(row_part, "col", distances("col")[level])
                if level < len(distances("row")):
                    col_other = partner(col_part, "row", distances("row")[level])
                yield [row_part, col_part], 1
                row_part, col_part, row_other, col_other = settle(
                    (row_part, col_part, row_other, col_other)
                )
                row_part = row_part if row_other is None else row_part + row_other
                col_part = col_part if col_other is None else col_part + col_other
            packed = jnp.concatenate(
                [
                    jnp.where(place == last, row_part, 0.0),
                    jnp.where(place == 0, row_part, 0.0),
                    jnp.where(at_end, col_part, 0.0),
                ]
            )
            far = lax.ppermute(packed, "dp", [(0, last), (last, 0)])
            yield [packed], FAR
            packed, far = settle((packed, far))

            row_new, col_new = factors(m, packed + far)
            row_scale = lax.rsqrt(jnp.where(place == 0, row_new[half:], row_new[:half]))
            col_scale = lax.rsqrt(col_new)
            energy = None
            for g in range(GROUPS):
                low, high = g * half // GROUPS, (g + 1) * half // GROUPS
                wide = settle(total)[low:high].astype(F32)
                raw = wide * row_scale[low:high, None] * col_scale[None, :]
                part = jnp.sum(raw * raw)
                energy = part if energy is None else energy + part
            energy = jnp.broadcast_to(energy, (8, LANES))
            for axis in ("col", "row"):
                for distance in distances(axis):
                    other = partner(energy, axis, distance)
                    yield [energy], 1
                    energy, other = settle((energy, other))
                    energy = energy + other
            other = lax.ppermute(energy, "dp", [(0, last), (last, 0)])
            yield [energy], FAR + m
            energy, other = settle((energy, other))
            energy = (energy + other)[0, 0]
            rms = jnp.sqrt(energy / (rows * n_row * cols * n_col))
            row_final = row_scale / jnp.maximum(1.0, rms)
            scales[m] = [
                total,
                jnp.broadcast_to(row_final[:, None], (half, LANES)),
                jnp.broadcast_to(col_scale[None, :], (8, cols)),
            ]
            sums[m] = (packed, far)
            yield [scales[m][1], scales[m][2]], steps

        def factors(m, total):
            rows, cols = shapes[m]
            row_new = BETA * prevs[m][0] + (1.0 - BETA) * (total[:rows] / (cols * n_col))
            col_new = BETA * prevs[m][1] + (1.0 - BETA) * (total[rows:] / (rows * n_row))
            return row_new, col_new

        def closing():
            packed, far = (jnp.concatenate([sums[m][k] for m in range(2)]) for k in range(2))
            total = packed + far
            for j in range(1, last):
                for pairs in (
                    [[(0, j), (last, last - j)]] if j != last - j else [[(0, j)], [(last, j)]]
                ):
                    got = lax.ppermute(settle(packed), "dp", pairs)
                    yield [total], FAR
                    total = total + settle(got)
            cut = sum(shapes[0])
            results[0] = factors(0, total[:cut])
            results[1] = factors(1, total[cut:])
            yield [*results[0], *results[1]], steps

        workers = [statistics(0), statistics(1), closing()]
        wakes = [0, 0, messages - 2]
        outs = [None, None]
        inflight = {}
        tied = []
        for s in range(steps):
            before, tied = tied, []
            movers = [p for p in range(n_dp) if 0 <= s - LAG * p < messages]
            parts = []
            for index, (kind, m) in enumerate(kinds):
                begin = index * count
                members = [p for p in movers if begin <= s - LAG * p < begin + count]
                if not members:
                    continue
                part = dict(kind=kind, m=m, begin=begin, shape=shapes[m])
                if kind == "sum":
                    part["chunk"] = s - begin - LAG * last if last in members else None
                    part.update(grad=grads[m], state=states[m])
                else:
                    while m not in scales:
                        wakes[m] = s + next(workers[m])[1]
                    part["chunk"] = s - begin if 0 in members else None
                    part.update(scales=scales[m], out=outs[m])
                parts.append(part)
            gots = inflight.pop(s - LAG, None)
            sending = min(movers) < last
            values, given = run_step(here, s, count, last, gots, parts, message, sending)
            for part, made in zip(parts, given):
                if part["kind"] == "spread":
                    outs[part["m"]] = made[0]
                elif made:
                    states[part["m"]] = made
                    finished[part["m"]] += 1
            if sending:
                tied, _ = lax.optimization_barrier((values, (before, gots)))
                tied = list(tied)
                going = [p for p in movers if p < last]
                inflight[s] = [
                    lax.ppermute(tied[0], "dp", [(p, p + 1) for p in going]),
                    lax.ppermute(tied[1], "dp", [(last - p, last - p - 1) for p in going]),
                ]
                cell[0] = list(tied)
            for w, worker in enumerate(workers):
                if s >= wakes[w]:
                    ties, wait = next(worker)
                    tied = tied + ties
                    wakes[w] = s + wait
        while not results:
            next(workers[2])
        return (outs[0], *results[0], outs[1], *results[1])

    return local


def solution(mesh):
    return jax.shard_map(
        make_local(dict(mesh.shape)),
        mesh=mesh,
        in_specs=(
            P("dp", "row", "col"),
            P("dp", "row", "col"),
            P("row"),
            P("col"),
            P("row"),
            P("col"),
        ),
        out_specs=(P("row", "col"), P("row"), P("col"), P("row", "col"), P("row"), P("col")),
        check_vma=False,
    )
```

```python
import functools

import jax
import jax.numpy as jnp
from jax import lax
from jax.experimental import pallas as pl
from jax.experimental.pallas import tpu as pltpu
from jax.sharding import PartitionSpec as P

BETA = 0.8
EPS_SQUARE = 1e-30
CHUNKS = 16
LAG = 2
GROUPS = 4
FAR = 2
LANES = 128
PIECE = 16384
VMEM_BYTES = 48 * 1024 * 1024

F32 = jnp.float32
BF16 = jnp.bfloat16
ANY = pl.BlockSpec(memory_space=pl.ANY)


def chunk_count(shapes):
    count = CHUNKS
    while any(rows % (32 * count) for rows, _ in shapes):
        count //= 2
    return count


def step_kernel(plan, place_ref, *refs):
    refs = list(refs)
    gots = [refs.pop(0), refs.pop(0)] if plan["with_got"] else [None, None]
    taken = []
    for part in plan["parts"]:
        taken.append([refs.pop(0) for _ in range(part["operands"])])
    sends = [refs.pop(0), refs.pop(0)] if plan["sending"] else [None, None]
    given = []
    for part in plan["parts"]:
        given.append([refs.pop(0) for _ in range(part["results"])])
    (sems,) = refs

    place, last, count = place_ref[0], plan["last"], plan["count"]
    numbers = [plan["step"] - LAG * place, plan["step"] - LAG * (last - place)]
    positions = [place, last - place]

    def each_piece(size, q, width, body, carry=0):
        step = min(width, max(LANES, PIECE // size // LANES * LANES))
        across = width // step

        def turn(t, carry):
            at = pl.ds(pl.multiple_of(t // across * size, 16), size)
            lanes = pl.ds(pl.multiple_of(t % across * step, LANES), step)
            return body(at, lanes, pl.ds(pl.multiple_of(t * step, LANES), step), carry)

        return lax.fori_loop(0, q * across, turn, carry)

    for part, ins, outs in zip(plan["parts"], taken, given):
        size, q, width, begin = part["size"], part["q"], part["width"], part["begin"]
        here = [n - begin for n in numbers]
        valids = [(n >= 0) & (n < count) for n in here]
        if part["kind"] == "sum":
            def add(d, at, lanes, full):
                value = ins[d][:, full]
                if plan["with_got"]:
                    value = (gots[d][at, lanes].astype(F32) + value.astype(F32)).astype(BF16)
                sends[d][at, lanes] = value
                return value

            for d in range(2):
                ending = (place == (last, 0)[d]) & (part["chunk"] is not None)

                @pl.when(valids[d] & jnp.logical_not(ending))
                def _():
                    def pass_on(at, lanes, full, carry):
                        add(d, at, lanes, full)
                        return carry

                    each_piece(size, q, width, pass_on)

                if part["chunk"] is not None:
                    total_ref, row_ref, col_ref = outs

                    @pl.when(ending)
                    def _():
                        def measure(at, lanes, full, row_part):
                            total = add(d, at, lanes, full)
                            total_ref[:, full] = total
                            wide = total.astype(F32)
                            square = wide * wide + EPS_SQUARE
                            for lane in range(0, square.shape[1], LANES):
                                row_part = row_part + square[:, lane : lane + LANES]
                            col_part = square[0:8]
                            for r in range(8, size, 8):
                                col_part = col_part + square[r : r + 8]
                            if not part["first"]:
                                col_part = col_part + ins[-1][:, full]
                            col_ref[:, full] = col_part
                            return row_part

                        row_ref[...] = each_piece(
                            size, q, width, measure, jnp.zeros((size, LANES), F32)
                        )

        else:
            out_ref = outs[0]

            def keep(source, d, j):
                row = ((1 - d) * count + jnp.clip(here[d], 0, count - 1)) * size
                return pltpu.make_async_copy(
                    source.at[pl.ds(j * size, size), :],
                    out_ref.at[pl.ds(pl.multiple_of(row, 16), size), pl.ds(j * width, width)],
                    sems.at[d, j],
                )

            for d in range(2):
                if part["chunk"] is not None:
                    total_ref, row_ref, col_ref = ins[:3]

                    @pl.when(valids[d] & (positions[d] == 0))
                    def _():
                        def scale(at, lanes, full, carry):
                            wide = total_ref[:, full].astype(F32)
                            rows = jnp.concatenate([row_ref[...]] * (wide.shape[1] // LANES), axis=1)
                            update = wide * rows * col_ref[0:1, full]
                            sends[d][at, lanes] = update.astype(BF16)
                            return carry

                        each_piece(size, q, width, scale)
                        for j in range(q):
                            keep(sends[d], d, j).start()

                if plan["with_got"]:

                    @pl.when(valids[d] & (positions[d] > 0))
                    def _():
                        for j in range(q):
                            keep(gots[d], d, j).start()
                        if plan["sending"]:
                            def forward(at, lanes, full, carry):
                                sends[d][at, lanes] = gots[d][at, lanes]
                                return carry

                            each_piece(size, q, width, forward)

            for d in range(2):

                @pl.when(valids[d])
                def _():
                    for j in range(q):
                        keep(gots[d] if sends[d] is None else sends[d], d, j).wait()


def run_step(place, s, count, last, gots, parts, message, sending):
    window = pl.BlockSpec(message, lambda i, at: (0, 0))
    operands, in_specs, out_shape, out_specs, aliases = [], [], [], [], {}
    with_got = gots is not None
    if with_got:
        operands += gots
        in_specs += [window, window]
    if sending:
        out_shape += [jax.ShapeDtypeStruct(message, BF16)] * 2
        out_specs += [window, window]
    plans = []
    widest = 1
    for part in parts:
        rows, cols = part["shape"]
        half, size = rows // 2, rows // 2 // count
        q, width = cols // message[1], message[1]
        widest = max(widest, q)
        chunk = part["chunk"]
        block = pl.BlockSpec((size, cols), lambda i, at, k=chunk: (k, 0))
        lanes = pl.BlockSpec((size, LANES), lambda i, at, k=chunk: (k, 0))
        whole = pl.BlockSpec((8, cols), lambda i, at: (0, 0))
        before, results_before = len(operands), len(out_shape)
        if part["kind"] == "sum":
            for d in range(2):

                def from_grad(i, at, d=d, begin=part["begin"]):
                    number = s - begin - LAG * (at[0] if d == 0 else last - at[0])
                    return (d * count + jnp.clip(number, 0, count - 1), 0)

                operands.append(part["grad"])
                in_specs.append(pl.BlockSpec((size, cols), from_grad))
            if chunk is not None:
                if part["state"] is not None:
                    for k in range(3):
                        aliases[len(operands) + 1 + k] = len(out_shape) + k
                    operands += part["state"]
                    in_specs += [ANY, ANY, whole]
                out_shape += [
                    jax.ShapeDtypeStruct((half, cols), BF16),
                    jax.ShapeDtypeStruct((half, LANES), F32),
                    jax.ShapeDtypeStruct((8, cols), F32),
                ]
                out_specs += [block, lanes, whole]
        else:
            if chunk is not None:
                operands += part["scales"]
                in_specs += [block, lanes, whole]
            if part["out"] is not None:
                aliases[len(operands) + 1] = len(out_shape)
                operands.append(part["out"])
                in_specs.append(ANY)
            out_shape.append(jax.ShapeDtypeStruct((rows, cols), BF16))
            out_specs.append(ANY)
        plans.append(
            dict(
                kind=part["kind"],
                begin=part["begin"],
                chunk=chunk,
                first=part.get("state") is None,
                size=size,
                q=q,
                width=width,
                operands=len(operands) - before,
                results=len(out_shape) - results_before,
            )
        )
    plan = dict(
        step=s, count=count, last=last, with_got=with_got, sending=sending, parts=plans
    )
    elements = message[0] * message[1]
    out = pl.pallas_call(
        functools.partial(step_kernel, plan),
        grid_spec=pltpu.PrefetchScalarGridSpec(
            num_scalar_prefetch=1,
            grid=(1,),
            in_specs=in_specs,
            out_specs=out_specs,
            scratch_shapes=[pltpu.SemaphoreType.DMA((2, widest))],
        ),
        out_shape=out_shape,
        input_output_aliases=aliases,
        compiler_params=pltpu.CompilerParams(vmem_limit_bytes=VMEM_BYTES),
        cost_estimate=pl.CostEstimate(
            flops=4 * elements, bytes_accessed=12 * elements, transcendentals=0
        ),
        name="line_step",
    )(place, *operands)
    out = list(out)
    values = [out.pop(0), out.pop(0)] if sending else None
    return values, [[out.pop(0) for _ in range(plan["results"])] for plan in plans]


def make_local(axis_sizes):
    n_dp, n_row, n_col = axis_sizes["dp"], axis_sizes["row"], axis_sizes["col"]
    last = n_dp - 1

    def partner(value, axis, distance):
        n = axis_sizes[axis]
        return lax.ppermute(value, axis, [(i, i ^ distance) for i in range(n)])

    def distances(axis):
        out, d = [], 1
        while d < axis_sizes[axis]:
            out.append(d)
            d *= 2
        return out

    def local(grad_wi, grad_wo, row_wi, col_wi, row_wo, col_wo):
        place = lax.axis_index("dp")
        grads = (grad_wi[0], grad_wo[0])
        prevs = ((row_wi, col_wi), (row_wo, col_wo))
        shapes = [g.shape for g in grads]
        count = chunk_count(shapes)
        here = place[None].astype(jnp.int32)
        at_end = (place == last) | (place == 0)
        width = min(cols for _, cols in shapes)
        message = (shapes[0][0] * shapes[0][1] // (2 * count * width), width)

        kinds = [("sum", 0), ("sum", 1), ("spread", 0), ("spread", 1)]
        messages = len(kinds) * count
        steps = messages + LAG * last

        states = [None, None]
        finished = [0, 0]
        scales = {}
        results = {}
        sums = {}
        cell = [None]

        def settle(value):
            value, _ = lax.optimization_barrier((value, cell[0]))
            return value

        def statistics(m):
            rows, cols = shapes[m]
            half = rows // 2
            while finished[m] < count:
                yield [], 1
            total, row_lanes, col_rows = states[m]
            row_part = jnp.sum(row_lanes, axis=1)
            col_part = jnp.sum(col_rows, axis=0)
            levels = max(len(distances("row")), len(distances("col")))
            for level in range(levels):
                row_other = col_other = None
                if level < len(distances("col")):
                    row_other = partner(row_part, "col", distances("col")[level])
                if level < len(distances("row")):
                    col_other = partner(col_part, "row", distances("row")[level])
                yield [row_part, col_part], 1
                row_part, col_part, row_other, col_other = settle(
                    (row_part, col_part, row_other, col_other)
                )
                row_part = row_part if row_other is None else row_part + row_other
                col_part = col_part if col_other is None else col_part + col_other
            packed = jnp.concatenate(
                [
                    jnp.where(place == last, row_part, 0.0),
                    jnp.where(place == 0, row_part, 0.0),
                    jnp.where(at_end, col_part, 0.0),
                ]
            )
            far = lax.ppermute(packed, "dp", [(0, last), (last, 0)])
            yield [packed], FAR
            packed, far = settle((packed, far))

            row_new, col_new = factors(m, packed + far)
            row_scale = lax.rsqrt(jnp.where(place == 0, row_new[half:], row_new[:half]))
            col_scale = lax.rsqrt(col_new)
            energy = None
            for g in range(GROUPS):
                low, high = g * half // GROUPS, (g + 1) * half // GROUPS
                wide = settle(total)[low:high].astype(F32)
                raw = wide * row_scale[low:high, None] * col_scale[None, :]
                part = jnp.sum(raw * raw)
                energy = part if energy is None else energy + part
            energy = jnp.broadcast_to(energy, (8, LANES))
            for axis in ("col", "row"):
                for distance in distances(axis):
                    other = partner(energy, axis, distance)
                    yield [energy], 1
                    energy, other = settle((energy, other))
                    energy = energy + other
            other = lax.ppermute(energy, "dp", [(0, last), (last, 0)])
            yield [energy], FAR + m
            energy, other = settle((energy, other))
            energy = (energy + other)[0, 0]
            rms = jnp.sqrt(energy / (rows * n_row * cols * n_col))
            row_final = row_scale / jnp.maximum(1.0, rms)
            scales[m] = [
                total,
                jnp.broadcast_to(row_final[:, None], (half, LANES)),
                jnp.broadcast_to(col_scale[None, :], (8, cols)),
            ]
            sums[m] = (packed, far)
            yield [scales[m][1], scales[m][2]], steps

        def factors(m, total):
            rows, cols = shapes[m]
            row_new = BETA * prevs[m][0] + (1.0 - BETA) * (total[:rows] / (cols * n_col))
            col_new = BETA * prevs[m][1] + (1.0 - BETA) * (total[rows:] / (rows * n_row))
            return row_new, col_new

        def closing():
            packed, far = (jnp.concatenate([sums[m][k] for m in range(2)]) for k in range(2))
            total = packed + far
            for j in range(1, last):
                for pairs in (
                    [[(0, j), (last, last - j)]] if j != last - j else [[(0, j)], [(last, j)]]
                ):
                    got = lax.ppermute(settle(packed), "dp", pairs)
                    yield [total], FAR
                    total = total + settle(got)
            cut = sum(shapes[0])
            results[0] = factors(0, total[:cut])
            results[1] = factors(1, total[cut:])
            yield [*results[0], *results[1]], steps

        workers = [statistics(0), statistics(1), closing()]
        wakes = [0, 0, messages - 2]
        outs = [None, None]
        inflight = {}
        tied = []
        for s in range(steps):
            before, tied = tied, []
            movers = [p for p in range(n_dp) if 0 <= s - LAG * p < messages]
            parts = []
            for index, (kind, m) in enumerate(kinds):
                begin = index * count
                members = [p for p in movers if begin <= s - LAG * p < begin + count]
                if not members:
                    continue
                part = dict(kind=kind, m=m, begin=begin, shape=shapes[m])
                if kind == "sum":
                    part["chunk"] = s - begin - LAG * last if last in members else None
                    part.update(grad=grads[m], state=states[m])
                else:
                    while m not in scales:
                        wakes[m] = s + next(workers[m])[1]
                    part["chunk"] = s - begin if 0 in members else None
                    part.update(scales=scales[m], out=outs[m])
                parts.append(part)
            gots = inflight.pop(s - LAG, None)
            sending = min(movers) < last
            values, given = run_step(here, s, count, last, gots, parts, message, sending)
            for part, made in zip(parts, given):
                if part["kind"] == "spread":
                    outs[part["m"]] = made[0]
                elif made:
                    states[part["m"]] = made
                    finished[part["m"]] += 1
            if sending:
                tied, _ = lax.optimization_barrier((values, (before, gots)))
                tied = list(tied)
                going = [p for p in movers if p < last]
                inflight[s] = [
                    lax.ppermute(tied[0], "dp", [(p, p + 1) for p in going]),
                    lax.ppermute(tied[1], "dp", [(last - p, last - p - 1) for p in going]),
                ]
                cell[0] = list(tied)
            for w, worker in enumerate(workers):
                if s >= wakes[w]:
                    ties, wait = next(worker)
                    tied = tied + ties
                    wakes[w] = s + wait
        while not results:
            next(workers[2])
        return (outs[0], *results[0], outs[1], *results[1])

    return local


def solution(mesh):
    return jax.shard_map(
        make_local(dict(mesh.shape)),
        mesh=mesh,
        in_specs=(
            P("dp", "row", "col"),
            P("dp", "row", "col"),
            P("row"),
            P("col"),
            P("row"),
            P("col"),
        ),
        out_specs=(P("row", "col"), P("row"), P("col"), P("row", "col"), P("row"), P("col")),
        check_vma=False,
    )
```

```python
import functools

import jax
import jax.numpy as jnp
from jax import lax
from jax.experimental import pallas as pl
from jax.experimental.pallas import tpu as pltpu
from jax.sharding import PartitionSpec as P

BETA = 0.8
EPS_SQUARE = 1e-30
CHUNKS = 16
LAG = 2
GROUPS = 1
FAR = 2
LANES = 128
PIECE = 16384
VMEM_BYTES = 48 * 1024 * 1024

F32 = jnp.float32
BF16 = jnp.bfloat16
ANY = pl.BlockSpec(memory_space=pl.ANY)


def chunk_count(shapes):
    count = CHUNKS
    while any(rows % (32 * count) for rows, _ in shapes):
        count //= 2
    return count


def step_kernel(plan, place_ref, *refs):
    refs = list(refs)
    gots = [refs.pop(0), refs.pop(0)] if plan["with_got"] else [None, None]
    taken = []
    for part in plan["parts"]:
        taken.append([refs.pop(0) for _ in range(part["operands"])])
    sends = [refs.pop(0), refs.pop(0)] if plan["sending"] else [None, None]
    given = []
    for part in plan["parts"]:
        given.append([refs.pop(0) for _ in range(part["results"])])
    (sems,) = refs

    place, last, count = place_ref[0], plan["last"], plan["count"]
    numbers = [plan["step"] - LAG * place, plan["step"] - LAG * (last - place)]
    positions = [place, last - place]

    def each_piece(size, q, width, body, carry=0):
        step = min(width, max(LANES, PIECE // size // LANES * LANES))
        across = width // step

        def turn(t, carry):
            at = pl.ds(pl.multiple_of(t // across * size, 16), size)
            lanes = pl.ds(pl.multiple_of(t % across * step, LANES), step)
            return body(at, lanes, pl.ds(pl.multiple_of(t * step, LANES), step), carry)

        return lax.fori_loop(0, q * across, turn, carry)

    for part, ins, outs in zip(plan["parts"], taken, given):
        size, q, width, begin = part["size"], part["q"], part["width"], part["begin"]
        here = [n - begin for n in numbers]
        valids = [(n >= 0) & (n < count) for n in here]
        if part["kind"] == "sum":
            def add(d, at, lanes, full):
                value = ins[d][:, full]
                if plan["with_got"]:
                    value = (gots[d][at, lanes].astype(F32) + value.astype(F32)).astype(BF16)
                sends[d][at, lanes] = value
                return value

            for d in range(2):
                ending = (place == (last, 0)[d]) & (part["chunk"] is not None)

                @pl.when(valids[d] & jnp.logical_not(ending))
                def _():
                    def pass_on(at, lanes, full, carry):
                        add(d, at, lanes, full)
                        return carry

                    each_piece(size, q, width, pass_on)

                if part["chunk"] is not None:
                    total_ref, row_ref, col_ref = outs

                    @pl.when(ending)
                    def _():
                        def measure(at, lanes, full, row_part):
                            total = add(d, at, lanes, full)
                            total_ref[:, full] = total
                            wide = total.astype(F32)
                            square = wide * wide + EPS_SQUARE
                            for lane in range(0, square.shape[1], LANES):
                                row_part = row_part + square[:, lane : lane + LANES]
                            col_part = square[0:8]
                            for r in range(8, size, 8):
                                col_part = col_part + square[r : r + 8]
                            if not part["first"]:
                                col_part = col_part + ins[-1][:, full]
                            col_ref[:, full] = col_part
                            return row_part

                        row_ref[...] = each_piece(
                            size, q, width, measure, jnp.zeros((size, LANES), F32)
                        )

        else:
            out_ref = outs[0]

            def keep(source, d, j):
                row = ((1 - d) * count + jnp.clip(here[d], 0, count - 1)) * size
                return pltpu.make_async_copy(
                    source.at[pl.ds(j * size, size), :],
                    out_ref.at[pl.ds(pl.multiple_of(row, 16), size), pl.ds(j * width, width)],
                    sems.at[d, j],
                )

            for d in range(2):
                if part["chunk"] is not None:
                    total_ref, row_ref, col_ref = ins[:3]

                    @pl.when(valids[d] & (positions[d] == 0))
                    def _():
                        def scale(at, lanes, full, carry):
                            wide = total_ref[:, full].astype(F32)
                            rows = jnp.concatenate([row_ref[...]] * (wide.shape[1] // LANES), axis=1)
                            update = wide * rows * col_ref[0:1, full]
                            sends[d][at, lanes] = update.astype(BF16)
                            return carry

                        each_piece(size, q, width, scale)
                        for j in range(q):
                            keep(sends[d], d, j).start()

                if plan["with_got"]:

                    @pl.when(valids[d] & (positions[d] > 0))
                    def _():
                        for j in range(q):
                            keep(gots[d], d, j).start()
                        if plan["sending"]:
                            def forward(at, lanes, full, carry):
                                sends[d][at, lanes] = gots[d][at, lanes]
                                return carry

                            each_piece(size, q, width, forward)

            for d in range(2):

                @pl.when(valids[d])
                def _():
                    for j in range(q):
                        keep(gots[d] if sends[d] is None else sends[d], d, j).wait()


def run_step(place, s, count, last, gots, parts, message, sending):
    window = pl.BlockSpec(message, lambda i, at: (0, 0))
    operands, in_specs, out_shape, out_specs, aliases = [], [], [], [], {}
    with_got = gots is not None
    if with_got:
        operands += gots
        in_specs += [window, window]
    if sending:
        out_shape += [jax.ShapeDtypeStruct(message, BF16)] * 2
        out_specs += [window, window]
    plans = []
    widest = 1
    for part in parts:
        rows, cols = part["shape"]
        half, size = rows // 2, rows // 2 // count
        q, width = cols // message[1], message[1]
        widest = max(widest, q)
        chunk = part["chunk"]
        block = pl.BlockSpec((size, cols), lambda i, at, k=chunk: (k, 0))
        lanes = pl.BlockSpec((size, LANES), lambda i, at, k=chunk: (k, 0))
        whole = pl.BlockSpec((8, cols), lambda i, at: (0, 0))
        before, results_before = len(operands), len(out_shape)
        if part["kind"] == "sum":
            for d in range(2):

                def from_grad(i, at, d=d, begin=part["begin"]):
                    number = s - begin - LAG * (at[0] if d == 0 else last - at[0])
                    return (d * count + jnp.clip(number, 0, count - 1), 0)

                operands.append(part["grad"])
                in_specs.append(pl.BlockSpec((size, cols), from_grad))
            if chunk is not None:
                if part["state"] is not None:
                    for k in range(3):
                        aliases[len(operands) + 1 + k] = len(out_shape) + k
                    operands += part["state"]
                    in_specs += [ANY, ANY, whole]
                out_shape += [
                    jax.ShapeDtypeStruct((half, cols), BF16),
                    jax.ShapeDtypeStruct((half, LANES), F32),
                    jax.ShapeDtypeStruct((8, cols), F32),
                ]
                out_specs += [block, lanes, whole]
        else:
            if chunk is not None:
                operands += part["scales"]
                in_specs += [block, lanes, whole]
            if part["out"] is not None:
                aliases[len(operands) + 1] = len(out_shape)
                operands.append(part["out"])
                in_specs.append(ANY)
            out_shape.append(jax.ShapeDtypeStruct((rows, cols), BF16))
            out_specs.append(ANY)
        plans.append(
            dict(
                kind=part["kind"],
                begin=part["begin"],
                chunk=chunk,
                first=part.get("state") is None,
                size=size,
                q=q,
                width=width,
                operands=len(operands) - before,
                results=len(out_shape) - results_before,
            )
        )
    plan = dict(
        step=s, count=count, last=last, with_got=with_got, sending=sending, parts=plans
    )
    elements = message[0] * message[1]
    out = pl.pallas_call(
        functools.partial(step_kernel, plan),
        grid_spec=pltpu.PrefetchScalarGridSpec(
            num_scalar_prefetch=1,
            grid=(1,),
            in_specs=in_specs,
            out_specs=out_specs,
            scratch_shapes=[pltpu.SemaphoreType.DMA((2, widest))],
        ),
        out_shape=out_shape,
        input_output_aliases=aliases,
        compiler_params=pltpu.CompilerParams(vmem_limit_bytes=VMEM_BYTES),
        cost_estimate=pl.CostEstimate(
            flops=4 * elements, bytes_accessed=12 * elements, transcendentals=0
        ),
        name="line_step",
    )(place, *operands)
    out = list(out)
    values = [out.pop(0), out.pop(0)] if sending else None
    return values, [[out.pop(0) for _ in range(plan["results"])] for plan in plans]


def make_local(axis_sizes):
    n_dp, n_row, n_col = axis_sizes["dp"], axis_sizes["row"], axis_sizes["col"]
    last = n_dp - 1

    def partner(value, axis, distance):
        n = axis_sizes[axis]
        return lax.ppermute(value, axis, [(i, i ^ distance) for i in range(n)])

    def distances(axis):
        out, d = [], 1
        while d < axis_sizes[axis]:
            out.append(d)
            d *= 2
        return out

    def local(grad_wi, grad_wo, row_wi, col_wi, row_wo, col_wo):
        place = lax.axis_index("dp")
        grads = (grad_wi[0], grad_wo[0])
        prevs = ((row_wi, col_wi), (row_wo, col_wo))
        shapes = [g.shape for g in grads]
        count = chunk_count(shapes)
        here = place[None].astype(jnp.int32)
        at_end = (place == last) | (place == 0)
        width = min(cols for _, cols in shapes)
        message = (shapes[0][0] * shapes[0][1] // (2 * count * width), width)

        kinds = [("sum", 0), ("sum", 1), ("spread", 0), ("spread", 1)]
        messages = len(kinds) * count
        steps = messages + LAG * last

        states = [None, None]
        finished = [0, 0]
        scales = {}
        results = {}
        sums = {}
        cell = [None]

        def settle(value):
            value, _ = lax.optimization_barrier((value, cell[0]))
            return value

        def statistics(m):
            rows, cols = shapes[m]
            half = rows // 2
            while finished[m] < count:
                yield [], 1
            total, row_lanes, col_rows = states[m]
            row_part = jnp.sum(row_lanes, axis=1)
            col_part = jnp.sum(col_rows, axis=0)
            levels = max(len(distances("row")), len(distances("col")))
            for level in range(levels):
                row_other = col_other = None
                if level < len(distances("col")):
                    row_other = partner(row_part, "col", distances("col")[level])
                if level < len(distances("row")):
                    col_other = partner(col_part, "row", distances("row")[level])
                yield [row_part, col_part], 1
                row_part, col_part, row_other, col_other = settle(
                    (row_part, col_part, row_other, col_other)
                )
                row_part = row_part if row_other is None else row_part + row_other
                col_part = col_part if col_other is None else col_part + col_other
            packed = jnp.concatenate(
                [
                    jnp.where(place == last, row_part, 0.0),
                    jnp.where(place == 0, row_part, 0.0),
                    jnp.where(at_end, col_part, 0.0),
                ]
            )
            far = lax.ppermute(packed, "dp", [(0, last), (last, 0)])
            yield [packed], FAR
            packed, far = settle((packed, far))

            row_new, col_new = factors(m, packed + far)
            row_scale = lax.rsqrt(jnp.where(place == 0, row_new[half:], row_new[:half]))
            col_scale = lax.rsqrt(col_new)
            energy = None
            for g in range(GROUPS):
                low, high = g * half // GROUPS, (g + 1) * half // GROUPS
                wide = settle(total)[low:high].astype(F32)
                raw = wide * row_scale[low:high, None] * col_scale[None, :]
                part = jnp.sum(raw * raw)
                energy = part if energy is None else energy + part
            energy = jnp.broadcast_to(energy, (8, LANES))
            for axis in ("col", "row"):
                for distance in distances(axis):
                    other = partner(energy, axis, distance)
                    yield [energy], 1
                    energy, other = settle((energy, other))
                    energy = energy + other
            other = lax.ppermute(energy, "dp", [(0, last), (last, 0)])
            yield [energy], FAR + m
            energy, other = settle((energy, other))
            energy = (energy + other)[0, 0]
            rms = jnp.sqrt(energy / (rows * n_row * cols * n_col))
            row_final = row_scale / jnp.maximum(1.0, rms)
            scales[m] = [
                total,
                jnp.broadcast_to(row_final[:, None], (half, LANES)),
                jnp.broadcast_to(col_scale[None, :], (8, cols)),
            ]
            sums[m] = (packed, far)
            yield [scales[m][1], scales[m][2]], steps

        def factors(m, total):
            rows, cols = shapes[m]
            row_new = BETA * prevs[m][0] + (1.0 - BETA) * (total[:rows] / (cols * n_col))
            col_new = BETA * prevs[m][1] + (1.0 - BETA) * (total[rows:] / (rows * n_row))
            return row_new, col_new

        def closing():
            packed, far = (jnp.concatenate([sums[m][k] for m in range(2)]) for k in range(2))
            total = packed + far
            for j in range(1, last):
                for pairs in (
                    [[(0, j), (last, last - j)]] if j != last - j else [[(0, j)], [(last, j)]]
                ):
                    got = lax.ppermute(settle(packed), "dp", pairs)
                    yield [total], FAR
                    total = total + settle(got)
            cut = sum(shapes[0])
            results[0] = factors(0, total[:cut])
            results[1] = factors(1, total[cut:])
            yield [*results[0], *results[1]], steps

        workers = [statistics(0), statistics(1), closing()]
        wakes = [0, 0, messages - 2]
        outs = [None, None]
        inflight = {}
        tied = []
        for s in range(steps):
            before, tied = tied, []
            movers = [p for p in range(n_dp) if 0 <= s - LAG * p < messages]
            parts = []
            for index, (kind, m) in enumerate(kinds):
                begin = index * count
                members = [p for p in movers if begin <= s - LAG * p < begin + count]
                if not members:
                    continue
                part = dict(kind=kind, m=m, begin=begin, shape=shapes[m])
                if kind == "sum":
                    part["chunk"] = s - begin - LAG * last if last in members else None
                    part.update(grad=grads[m], state=states[m])
                else:
                    while m not in scales:
                        wakes[m] = s + next(workers[m])[1]
                    part["chunk"] = s - begin if 0 in members else None
                    part.update(scales=scales[m], out=outs[m])
                parts.append(part)
            gots = inflight.pop(s - LAG, None)
            sending = min(movers) < last
            values, given = run_step(here, s, count, last, gots, parts, message, sending)
            for part, made in zip(parts, given):
                if part["kind"] == "spread":
                    outs[part["m"]] = made[0]
                elif made:
                    states[part["m"]] = made
                    finished[part["m"]] += 1
            if sending:
                tied, _ = lax.optimization_barrier((values, (before, gots)))
                tied = list(tied)
                going = [p for p in movers if p < last]
                inflight[s] = [
                    lax.ppermute(tied[0], "dp", [(p, p + 1) for p in going]),
                    lax.ppermute(tied[1], "dp", [(last - p, last - p - 1) for p in going]),
                ]
                cell[0] = list(tied)
            for w, worker in enumerate(workers):
                if s >= wakes[w]:
                    ties, wait = next(worker)
                    tied = tied + ties
                    wakes[w] = s + wait
        while not results:
            next(workers[2])
        return (outs[0], *results[0], outs[1], *results[1])

    return local


def solution(mesh):
    return jax.shard_map(
        make_local(dict(mesh.shape)),
        mesh=mesh,
        in_specs=(
            P("dp", "row", "col"),
            P("dp", "row", "col"),
            P("row"),
            P("col"),
            P("row"),
            P("col"),
        ),
        out_specs=(P("row", "col"), P("row"), P("col"), P("row", "col"), P("row"), P("col")),
        check_vma=False,
    )
```
